256 devices in a mesh: row: 8 (over z_hi, y), col: 32 (over z_lo, x, core).
Axes of the slice: x: 4, y: 4, z: 8 (z_hi: 2, z_lo: 4; z = z_hi * 4 + z_lo), core: 2. Of those that a mesh axis runs over, the one named last changes fastest.
Arguments:
- amplitudes: bfloat16 [4096, 512], P(('row', 'col')), may hold values from -6 to 6
- energies: float32 [4096, 512], P(('row', 'col')), may hold values from 0.5 to 4
- kernels: bfloat16 [6, 512, 512], replicated, may hold values from -0.25 to 0.25
- coefficients: bfloat16 [8, 32, 6, 1024, 512], P('row', 'col'), may hold values from -0.59765625 to 0.59765625
- target_block: int32 [8, 32, 6, 1024], P('row', 'col'), may hold values from 0 to 127
- source_block: int32 [8, 32, 6, 1024], P('row', 'col'), may hold values from 0 to 511
- slot_count: int32 [8, 32, 6], P('row', 'col'), may hold values from 204 to 1024, as said below
Outputs:
- product: float32 [4096, 512], P(('row', 'col'))
The draws below stay inside these ranges and needn't reach their ends.
Inputs may be any that keep to these rules, and one draw needn't show every extreme that they name: `slot_count`: in every draw some tile's list for some kernel is full, with 1024 used slots; the others hold between 204 and 1024.
All inputs are finite; a program needn't handle non-finite values.
Results may differ from the reference program's by a relative error of at most 0.0004.
Values may be sent and summed in bfloat16 or wider, within the bound.
A program may use at most 128 MiB of HBM per device.

```python
import math
import jax
import jax.numpy as jnp
from jax import lax

B = 512
PB = 16
NK = 6
CAPK = 1024
COLSEG = 128
ROWSEG = 512
NBLK = 4096
N_ROW = 8
N_COL = 32


def draw_slot_count(key, part):
    key = jax.random.fold_in(key, 7)
    first_key, second_key = jax.random.split(key)
    counts = jax.random.randint(first_key, (N_ROW * N_COL * NK,), CAPK // 5, CAPK + 1)
    chosen = jax.random.randint(second_key, (), 0, N_ROW * N_COL * NK)
    counts = jnp.where(jnp.arange(N_ROW * N_COL * NK) == chosen, CAPK, counts)
    return counts.reshape((N_ROW, N_COL, NK)).astype(jnp.int32)


def place_ends(values, own_key, smallest, largest):
    shape = values.shape
    spot = [jax.random.randint(jax.random.fold_in(own_key, axis), (), 0, shape[axis]) for axis in range(len(shape))]
    values = values.at[tuple(spot)].set(smallest)
    longest = shape.index(max(shape))
    spot[longest] = (spot[longest] + 1) % shape[longest]
    return values.at[tuple(spot)].set(largest)


def level_of(key, extent, cuts, low, largest):
    level = 1.0
    for axis_at, shards_of in cuts:
        draws = jax.random.uniform(jax.random.fold_in(jax.random.fold_in(key, 6), axis_at), (shards_of,), jnp.float32, low / len(cuts), largest / len(cuts))
        level = level * jnp.repeat(jnp.exp(draws), extent[axis_at] // shards_of).reshape((-1,) + (1,) * (len(extent) - 1 - axis_at))
    return level


def scatter_about(own_key, extent, spread, bound, shards=(), kind=jnp.bfloat16):
    result = spread * jax.random.normal(own_key, extent, jnp.float32)
    if shards:
        result = result * level_of(own_key, extent, shards, -0.22, 0.18)
    return jnp.clip(result, -bound, bound).astype(kind)


def setup_inputs(seed: int = 0) -> dict:
    keys = jax.random.split(jax.random.key(seed), 8)
    amplitudes = scatter_about(keys[0], (NBLK, B), 1.0, 6.0, ((0, 256),))
    energies = jnp.clip(jnp.exp(math.log(4.0) - 2.0794415 * jax.random.uniform(keys[1], (NBLK, B), jnp.float32) ** level_of(keys[1], (NBLK, B), ((0, 256),), -0.2, 0.2)), 0.5, 4.0)
    kernels = scatter_about(keys[2], (NK, B, B), B ** -0.5, 0.25)
    coefficients = scatter_about(keys[3], (N_ROW, N_COL, NK, CAPK, B), 0.1, 0.59765625, ((0, 8), (1, 32)))
    target_block = place_ends(jax.random.randint(keys[4], (N_ROW, N_COL, NK, CAPK), 0, COLSEG), jax.random.fold_in(keys[4], 1), 0, COLSEG - 1).astype(jnp.int32)
    source_block = place_ends(jax.random.randint(keys[5], (N_ROW, N_COL, NK, CAPK), 0, ROWSEG), jax.random.fold_in(keys[5], 1), 0, ROWSEG - 1).astype(jnp.int32)
    slot_count = draw_slot_count(jax.random.fold_in(keys[7], 71), 0)
    return {"amplitudes": amplitudes, "energies": energies, "kernels": kernels, "coefficients": coefficients, "target_block": target_block, "source_block": source_block, "slot_count": slot_count}


def reference(amplitudes, energies, kernels, coefficients, target_block, source_block, slot_count):
    flat_coef = coefficients.reshape((N_ROW * N_COL, NK, CAPK, B))
    flat_target = target_block.reshape((N_ROW * N_COL, NK, CAPK))
    flat_source = source_block.reshape((N_ROW * N_COL, NK, CAPK))
    flat_count = slot_count.reshape((N_ROW * N_COL, NK))
    slots = jnp.arange(CAPK, dtype=jnp.int32)
    wide_kernels = kernels.astype(jnp.float32)

    def one_tile(total, inputs):
        tile_id, coef_tile, target_tile, source_tile, count_tile = inputs
        row_id = (tile_id // N_COL).astype(jnp.int32)
        col_id = (tile_id % N_COL).astype(jnp.int32)
        for kernel_id in range(NK):
            in_use = (slots < count_tile[kernel_id]).astype(jnp.float32)
            weight = coef_tile[kernel_id].astype(jnp.float32) * in_use[:, None]
            local_target = target_tile[kernel_id]
            local_source = source_tile[kernel_id]
            global_target = (((local_target // PB) * N_COL + col_id) * PB + local_target % PB).astype(jnp.int32)
            global_source = (row_id * ROWSEG + local_source).astype(jnp.int32)
            picked = amplitudes[global_source]
            scaled = picked.astype(jnp.float32) * weight
            forward = jnp.dot(scaled, wide_kernels[kernel_id], precision=lax.Precision.HIGHEST)
            backward = lax.dot_general(amplitudes[global_target], kernels[kernel_id], (((1,), (1,)), ((), ())), preferred_element_type=jnp.float32)
            total = total.at[global_target].add(forward)
            total = total.at[global_source].add(backward * weight)
        return total, None

    start = energies * amplitudes.astype(jnp.float32)
    tiles = jnp.arange(N_ROW * N_COL, dtype=jnp.int32)
    total, unused = lax.scan(one_tile, start, (tiles, flat_coef, flat_target, flat_source, flat_count))
    return total
```

```python
import functools
import jax
import jax.numpy as jnp
from jax import lax
from jax.experimental import pallas as pl
from jax.experimental.pallas import tpu as pltpu
from jax.sharding import PartitionSpec as P

MESH = pl.DeviceIdType.MESH


def split(x):
    hi = x.astype(jnp.bfloat16)
    lo = (x - hi.astype(jnp.float32)).astype(jnp.bfloat16)
    return hi, lo


def onehot_rows(idx_row, count):
    slots = idx_row.shape[1]
    rows = lax.broadcasted_iota(jnp.int32, (count, slots), 0)
    return jnp.where(rows == idx_row, 1.0, 0.0).astype(jnp.bfloat16)


def onehot_cols(idx_row, count):
    slots = idx_row.shape[1]
    parts = []
    for at in range(0, slots, 128):
        wide = jnp.broadcast_to(idx_row[:, at:at + 128], (128, 128)).astype(jnp.float32).T
        tiles = []
        for base in range(0, count, 128):
            lanes = lax.broadcasted_iota(jnp.int32, (128, 128), 1).astype(jnp.float32) + float(base)
            tiles.append(jnp.where(lanes == wide, 1.0, 0.0).astype(jnp.bfloat16))
        parts.append(tiles[0] if len(tiles) == 1 else jnp.concatenate(tiles, axis=1))
    return jnp.concatenate(parts, axis=0)


def body(n_row, n_col, amp, coef, kern, tgt, src, cnt, out,
         coef_v, kern_v, row_seg, col_seg, row_part, col_part, row_recv, col_recv,
         load_sem, gather_row, gather_col, reduce_row, reduce_col, sent):
    r = lax.axis_index("row")
    c = lax.axis_index("col")
    nk, cap, states = coef_v.shape
    pb = amp.shape[0]
    n_src = n_col * pb
    n_tgt = n_row * pb
    f32 = jnp.float32

    def load(k):
        return (pltpu.make_async_copy(kern.at[k], kern_v.at[k], load_sem.at[0, k]),
                pltpu.make_async_copy(coef.at[k], coef_v.at[k], load_sem.at[1, k]))

    for k in range(nk):
        for copy in load(k):
            copy.start()

    barrier = pltpu.get_barrier_semaphore()

    def col_peer(d):
        return lax.rem(c + d, n_col)

    def row_peer(d):
        return lax.rem(r + d, n_row)

    def greet_row(d, z):
        pl.semaphore_signal(barrier, inc=1, device_id={"row": row_peer(d)}, device_id_type=MESH)
        return z

    def greet_col(d, z):
        pl.semaphore_signal(barrier, inc=1, device_id={"col": col_peer(d)}, device_id_type=MESH)
        return z

    lax.fori_loop(1, n_row, greet_row, 0)
    lax.fori_loop(1, n_col, greet_col, 0)
    pl.semaphore_wait(barrier, n_row + n_col - 2)

    own_row = pltpu.make_async_copy(amp, row_seg.at[pl.ds(pl.multiple_of(c * pb, pb), pb)], gather_row)
    own_col = pltpu.make_async_copy(amp, col_seg.at[pl.ds(pl.multiple_of(r * pb, pb), pb)], gather_col)
    own_col.start()
    own_row.start()

    def send_col_amp(d, z):
        pltpu.make_async_remote_copy(
            src_ref=amp, dst_ref=col_seg.at[pl.ds(pl.multiple_of(r * pb, pb), pb)],
            send_sem=sent.at[0], recv_sem=gather_col,
            device_id={"row": row_peer(d)}, device_id_type=MESH).start()
        return z

    def send_row_amp(d, z):
        pltpu.make_async_remote_copy(
            src_ref=amp, dst_ref=row_seg.at[pl.ds(pl.multiple_of(c * pb, pb), pb)],
            send_sem=sent.at[1], recv_sem=gather_row,
            device_id={"col": col_peer(d)}, device_id_type=MESH).start()
        return z

    lax.fori_loop(1, n_row, send_col_amp, 0)
    lax.fori_loop(1, n_col, send_row_amp, 0)

    row_part[...] = jnp.zeros_like(row_part)
    col_part[...] = jnp.zeros_like(col_part)

    pltpu.make_async_copy(col_seg, col_seg, gather_col).wait()

    def transposed(k, z):
        for copy in load(k):
            copy.wait()
        table = lax.dot_general(col_seg[...], kern_v[k], (((1,), (1,)), ((), ())), preferred_element_type=f32)
        hi, lo = split(table)
        both = jnp.concatenate([hi, lo], axis=0)
        slots = lax.broadcasted_iota(jnp.int32, (1, cap), 1)
        used = slots < cnt[k]
        tgt_row = jnp.where(used, tgt[pl.ds(k, 1), :], -1)
        src_row = jnp.where(used, src[pl.ds(k, 1), :], -1)
        pick = onehot_cols(tgt_row, n_tgt)
        picked = jnp.dot(jnp.concatenate([pick, pick], axis=1), both, preferred_element_type=f32)
        val_hi, val_lo = split(picked * coef_v[k].astype(f32))
        put = onehot_rows(src_row, n_src)
        row_part[...] += (jnp.dot(put, val_hi, preferred_element_type=f32)
                          + jnp.dot(put, val_lo, preferred_element_type=f32))
        return z

    lax.fori_loop(0, nk, transposed, 0)

    pltpu.make_async_copy(
        row_part.at[pl.ds(pl.multiple_of(c * pb, pb), pb)],
        row_recv.at[pl.ds(pl.multiple_of(c * pb, pb), pb)], reduce_row).start()

    def send_row_part(d, z):
        peer = col_peer(d)
        pltpu.make_async_remote_copy(
            src_ref=row_part.at[pl.ds(pl.multiple_of(peer * pb, pb), pb)],
            dst_ref=row_recv.at[pl.ds(pl.multiple_of(c * pb, pb), pb)],
            send_sem=sent.at[2], recv_sem=reduce_row,
            device_id={"col": peer}, device_id_type=MESH).start()
        return z

    lax.fori_loop(1, n_col, send_row_part, 0)

    pltpu.make_async_copy(row_seg, row_seg, gather_row).wait()

    def forward(k, z):
        slots = lax.broadcasted_iota(jnp.int32, (1, cap), 1)
        used = slots < cnt[k]
        tgt_row = jnp.where(used, tgt[pl.ds(k, 1), :], -1)
        src_row = jnp.where(used, src[pl.ds(k, 1), :], -1)
        pick = onehot_cols(src_row, n_src)
        picked = jnp.dot(pick, row_seg[...], preferred_element_type=f32)
        val_hi, val_lo = split(picked * coef_v[k].astype(f32))
        put = onehot_rows(tgt_row, n_tgt)
        total = (jnp.dot(put, val_hi, preferred_element_type=f32)
                 + jnp.dot(put, val_lo, preferred_element_type=f32))
        hi, lo = split(total)
        col_part[...] += (jnp.dot(hi, kern_v[k], preferred_element_type=f32)
                          + jnp.dot(lo, kern_v[k], preferred_element_type=f32))
        return z

    lax.fori_loop(0, nk, forward, 0)

    pltpu.make_async_copy(
        col_part.at[pl.ds(pl.multiple_of(r * pb, pb), pb)],
        col_recv.at[pl.ds(pl.multiple_of(r * pb, pb), pb)], reduce_col).start()

    def send_col_part(d, z):
        peer = row_peer(d)
        pltpu.make_async_remote_copy(
            src_ref=col_part.at[pl.ds(pl.multiple_of(peer * pb, pb), pb)],
            dst_ref=col_recv.at[pl.ds(pl.multiple_of(r * pb, pb), pb)],
            send_sem=sent.at[3], recv_sem=reduce_col,
            device_id={"row": peer}, device_id_type=MESH).start()
        return z

    lax.fori_loop(1, n_row, send_col_part, 0)

    pltpu.make_async_copy(row_recv, row_recv, reduce_row).wait()
    total = row_recv[pl.ds(0, pb)]
    for j in range(1, n_col):
        total = total + row_recv[pl.ds(j * pb, pb)]
    pltpu.make_async_copy(col_recv, col_recv, reduce_col).wait()
    for j in range(n_row):
        total = total + col_recv[pl.ds(j * pb, pb)]
    out[...] = total

    others_row = pl.ds(0, (n_row - 1) * pb)
    others_col = pl.ds(0, (n_col - 1) * pb)
    pltpu.make_async_copy(col_seg.at[others_row], col_seg.at[others_row], sent.at[0]).wait()
    pltpu.make_async_copy(row_seg.at[others_col], row_seg.at[others_col], sent.at[1]).wait()
    pltpu.make_async_copy(row_recv.at[others_col], row_recv.at[others_col], sent.at[2]).wait()
    pltpu.make_async_copy(col_recv.at[others_row], col_recv.at[others_row], sent.at[3]).wait()


def shards(amplitudes, energies, kernels, coefficients, target_block, source_block, slot_count):
    pb, states = amplitudes.shape
    n_row = lax.axis_size("row")
    n_col = lax.axis_size("col")
    nk, cap = coefficients.shape[2:4]
    vmem = pl.BlockSpec(memory_space=pltpu.VMEM)
    hbm = pl.BlockSpec(memory_space=pl.ANY)
    dma = pltpu.SemaphoreType.DMA
    bf16, f32 = jnp.bfloat16, jnp.float32
    total = pl.pallas_call(
        functools.partial(body, n_row, n_col),
        out_shape=jax.ShapeDtypeStruct((pb, states), f32),
        in_specs=[vmem, hbm, hbm, vmem, vmem, pl.BlockSpec(memory_space=pltpu.SMEM)],
        out_specs=vmem,
        scratch_shapes=[
            pltpu.VMEM((nk, cap, states), bf16),
            pltpu.VMEM((nk, states, states), bf16),
            pltpu.VMEM((n_col * pb, states), bf16),
            pltpu.VMEM((n_row * pb, states), bf16),
            pltpu.VMEM((n_col * pb, states), f32),
            pltpu.VMEM((n_row * pb, states), f32),
            pltpu.VMEM((n_col * pb, states), f32),
            pltpu.VMEM((n_row * pb, states), f32),
            dma((2, nk)), dma, dma, dma, dma, dma((4,)),
        ],
        compiler_params=pltpu.CompilerParams(
            collective_id=0, has_side_effects=True, vmem_limit_bytes=56 * 1024 * 1024),
        name="couplings",
    )(amplitudes, coefficients[0, 0], kernels, target_block[0, 0], source_block[0, 0], slot_count[0, 0])
    return total + energies * amplitudes.astype(f32)


def solution(mesh):
    in_specs = (
        P(("row", "col"), None),
        P(("row", "col"), None),
        P(),
        P("row", "col", None, None, None),
        P("row", "col", None, None),
        P("row", "col", None, None),
        P("row", "col", None),
    )
    out_specs = P(("row", "col"), None)
    return jax.shard_map(shards, mesh=mesh, in_specs=in_specs, out_specs=out_specs, check_vma=False)
```

```python
import functools
import jax
import jax.numpy as jnp
from jax import lax
from jax.experimental import pallas as pl
from jax.experimental.pallas import tpu as pltpu
from jax.sharding import PartitionSpec as P

MESH = pl.DeviceIdType.MESH
f32, bf16, i32, i16 = jnp.float32, jnp.bfloat16, jnp.int32, jnp.int16
LANES = 128


def split(x):
    hi = x.astype(bf16)
    return hi, (x - hi.astype(f32)).astype(bf16)


def dot(a, b):
    return jnp.dot(a, b, preferred_element_type=f32)


def encode(x):
    states = x.shape[1]
    top = jnp.maximum(jnp.max(jnp.abs(x), axis=1, keepdims=True), 1e-30)
    power = jnp.ceil(jnp.log2(jnp.broadcast_to(top, (x.shape[0], LANES)) * (1.0 / 32000.0)))
    scale = jnp.exp2(-power)
    parts = [jnp.round(x[:, at:at + LANES] * scale).astype(i32).astype(i16) for at in range(0, states, LANES)]
    return jnp.concatenate(parts + [power.astype(i32).astype(i16)], axis=1)


def decode(coded):
    states = coded.shape[1] - LANES
    scale = jnp.exp2(coded[:, states:].astype(i32).astype(f32))
    parts = [coded[:, at:at + LANES].astype(i32).astype(f32) * scale for at in range(0, states, LANES)]
    return jnp.concatenate(parts, axis=1)


def build(idx, cnt, k, rows_ref, cols_ref, count):
    one, zero = jnp.bfloat16(1), jnp.bfloat16(0)
    for m in range(idx.shape[0]):
        lane = lax.broadcasted_iota(i32, (1, LANES), 1) + m * LANES
        row = jnp.where(lane < cnt[k], idx[m:m + 1, :], -1)
        wide = jnp.broadcast_to(row, (LANES, LANES))
        down, across = wide.astype(i16), wide.T.astype(i16)
        for base in range(0, count, LANES):
            it = lax.broadcasted_iota(i16, (LANES, LANES), 0)
            rows_ref[k, pl.ds(base, LANES), pl.ds(m * LANES, LANES)] = jnp.where(it == down - jnp.int16(base), one, zero)
            it = lax.broadcasted_iota(i16, (LANES, LANES), 1)
            cols_ref[k, pl.ds(m * LANES, LANES), pl.ds(base, LANES)] = jnp.where(it == across - jnp.int16(base), one, zero)


def zip_run(*gens):
    gens = list(gens)
    while gens:
        for g in list(gens):
            try:
                next(g)
            except StopIteration:
                gens.remove(g)


def body(n_row, n_col, amp, coef, kern, tgt, src, cnt, out,
         coef_v, kern_v, row_seg, col_seg, row_part, col_part, sibling_part,
         row_code, row_land, col_code, col_land,
         t_pick, t_put, f_pick, f_put, hi_a, lo_a, hi_b, lo_b,
         load_sem, gather_row, gather_half, gather_col, cross, reduce_row, reduce_col, sent):
    r = lax.axis_index("row")
    c = lax.axis_index("col")
    core = lax.rem(c, 2)
    chip = lax.div(c, 2)
    chips = n_col // 2
    nk, cap, states = coef_v.shape
    pb = amp.shape[0]
    n_src, n_tgt = n_col * pb, n_row * pb
    half = n_src // 2
    groups = cap // LANES
    sibling = {"col": c + 1 - 2 * core}

    def piece(at):
        return pl.ds(pl.multiple_of(at * pb, pb), pb)

    def half_of(q):
        return pl.ds(pl.multiple_of(q * half, half), half)

    def load(k):
        return (pltpu.make_async_copy(kern.at[k], kern_v.at[k], load_sem.at[0, k]),
                pltpu.make_async_copy(coef.at[k], coef_v.at[k], load_sem.at[1, k]))

    def chip_peer(d):
        return lax.rem(chip + d, chips)

    def row_peer(d):
        return lax.rem(r + d, n_row)

    barrier = pltpu.get_barrier_semaphore()

    def greet_row(d, z):
        pl.semaphore_signal(barrier, inc=1, device_id={"row": row_peer(d)}, device_id_type=MESH)
        return z

    def greet_chip(d, z):
        pl.semaphore_signal(barrier, inc=1, device_id={"col": chip_peer(d) * 2 + core}, device_id_type=MESH)
        return z

    lax.fori_loop(1, n_row, greet_row, 0)
    lax.fori_loop(1, chips, greet_chip, 0)
    pl.semaphore_signal(barrier, inc=1, device_id=sibling, device_id_type=MESH)

    for k in range(nk):
        for copy in load(k):
            copy.start()
    own_row = pltpu.make_async_copy(amp, row_seg.at[piece(core * chips + chip)], gather_row)
    own_col = pltpu.make_async_copy(amp, col_seg.at[piece(r)], gather_col)
    own_col.start()
    own_row.start()

    pl.semaphore_wait(barrier, n_row + chips - 1)

    def send_col_amp(d, z):
        pltpu.make_async_remote_copy(
            src_ref=amp, dst_ref=col_seg.at[piece(r)], send_sem=sent.at[0], recv_sem=gather_col,
            device_id={"row": row_peer(d)}, device_id_type=MESH).start()
        return z

    def send_row_amp(d, z):
        pltpu.make_async_remote_copy(
            src_ref=amp, dst_ref=row_seg.at[piece(core * chips + chip)], send_sem=sent.at[1], recv_sem=gather_row,
            device_id={"col": chip_peer(d) * 2 + core}, device_id_type=MESH).start()
        return z

    lax.fori_loop(1, n_row, send_col_amp, 0)
    lax.fori_loop(1, chips, send_row_amp, 0)

    def build_both(k, z):
        at = pl.ds(pl.multiple_of(k * groups, groups), groups)
        build(tgt[at, :], cnt, k, f_put, t_pick, n_tgt)
        j = src[at, :]
        piece_of = lax.shift_right_logical(j, 4)
        spot = (piece_of & 1) * half + lax.shift_right_logical(piece_of, 1) * pb + (j & (pb - 1))
        build(spot, cnt, k, t_put, f_pick, n_src)
        return z

    lax.fori_loop(0, nk, build_both, 0)
    row_part[...] = jnp.zeros_like(row_part)
    col_part[...] = jnp.zeros_like(col_part)
    for k in range(nk):
        for copy in load(k):
            copy.wait()
    pltpu.make_async_copy(col_seg, col_seg, gather_col).wait()

    step = cap // 4

    def store_val(picked, k, at, hi, lo):
        h, l = split(picked * coef_v[k, pl.ds(at, step), :].astype(f32))
        hi[pl.ds(at, step), :] = h
        lo[pl.ds(at, step), :] = l

    def t_prep(k, hi, lo):
        table = lax.dot_general(col_seg[...], kern_v[k], (((1,), (1,)), ((), ())), preferred_element_type=f32)
        both = jnp.concatenate(split(table), axis=0)
        for at in range(0, cap, step):
            p = t_pick[k, pl.ds(at, step), :]
            store_val(dot(jnp.concatenate([p, p], axis=1), both), k, at, hi, lo)
            yield

    def t_fill(k, hi, lo):
        for at in range(0, states, 256):
            lanes = pl.ds(at, 256)
            p = t_put[k]
            row_part[:, lanes] += dot(p, hi[:, lanes]) + dot(p, lo[:, lanes])
            yield

    def f_prep(k, hi, lo):
        for at in range(0, cap, step):
            store_val(dot(f_pick[k, pl.ds(at, step), :], row_seg[...]), k, at, hi, lo)
            yield

    def f_fill(k, hi, lo):
        p = f_put[k]
        his, los = [], []
        for at in range(0, states, 256):
            lanes = pl.ds(at, 256)
            h, l = split(dot(p, hi[:, lanes]) + dot(p, lo[:, lanes]))
            his.append(h)
            los.append(l)
            yield
        h, l = jnp.concatenate(his, axis=1), jnp.concatenate(los, axis=1)
        for at in range(0, states, 256):
            lanes = pl.ds(at, 256)
            w = kern_v[k, :, lanes]
            col_part[:, lanes] += dot(h, w) + dot(l, w)
            yield

    a, b = (hi_a, lo_a), (hi_b, lo_b)
    bufs = [a, b]

    zip_run(t_prep(0, *a))
    zip_run(t_fill(0, *a), t_prep(1, *b))

    mine = half_of(core)
    pltpu.make_async_copy(row_seg.at[mine], row_seg.at[mine], gather_row).wait()
    hand = pltpu.make_async_remote_copy(
        src_ref=row_seg.at[mine], dst_ref=row_seg.at[mine], send_sem=sent.at[2], recv_sem=gather_half,
        device_id=sibling, device_id_type=MESH)
    hand.start()

    for k in range(1, nk - 1):
        zip_run(t_fill(k, *bufs[k % 2]), t_prep(k + 1, *bufs[(k + 1) % 2]))
    hand.wait()
    zip_run(t_fill(nk - 1, *bufs[(nk - 1) % 2]), f_prep(0, *bufs[nk % 2]))

    other = half_of(1 - core)
    swap = pltpu.make_async_remote_copy(
        src_ref=row_part.at[other], dst_ref=sibling_part, send_sem=sent.at[3], recv_sem=cross,
        device_id=sibling, device_id_type=MESH)
    swap.start()

    zip_run(f_fill(0, *bufs[nk % 2]), f_prep(1, *bufs[(nk + 1) % 2]))

    swap.wait()

    def code_row(i, z):
        at = pl.ds(pl.multiple_of(i * 64, 64), 64)
        total = row_part[pl.ds(pl.multiple_of(core * half + i * 64, 64), 64), :] + sibling_part[at, :]
        sibling_part[at, :] = total
        row_code[at, :] = encode(total)
        return z

    lax.fori_loop(0, half // 64, code_row, 0)

    def send_row(d, z):
        peer = chip_peer(d)
        pltpu.make_async_remote_copy(
            src_ref=row_code.at[piece(peer)], dst_ref=row_land.at[piece(chip)],
            send_sem=sent.at[4], recv_sem=reduce_row,
            device_id={"col": peer * 2 + core}, device_id_type=MESH).start()
        return z

    lax.fori_loop(1, chips, send_row, 0)
    own = pltpu.make_async_copy(row_code.at[piece(chip)], row_land.at[piece(chip)], reduce_row)
    own.start()

    for k in range(1, nk - 1):
        zip_run(f_fill(k, *bufs[(nk + k) % 2]), f_prep(k + 1, *bufs[(nk + k + 1) % 2]))
    zip_run(f_fill(nk - 1, *bufs[(2 * nk - 1) % 2]))

    col_code[...] = encode(col_part[...])

    def send_col(d, z):
        peer = row_peer(d)
        pltpu.make_async_remote_copy(
            src_ref=col_code.at[piece(peer)], dst_ref=col_land.at[piece(r)],
            send_sem=sent.at[5], recv_sem=reduce_col,
            device_id={"row": peer}, device_id_type=MESH).start()
        return z

    lax.fori_loop(1, n_row, send_col, 0)
    own = pltpu.make_async_copy(col_code.at[piece(r)], col_land.at[piece(r)], reduce_col)
    own.start()

    pltpu.make_async_copy(row_land, row_land, reduce_row).wait()
    total = decode(row_land[pl.ds(0, pb), :])
    for j in range(1, chips):
        total = total + decode(row_land[pl.ds(j * pb, pb), :])
    pltpu.make_async_copy(col_land, col_land, reduce_col).wait()
    for j in range(n_row):
        total = total + decode(col_land[pl.ds(j * pb, pb), :])
    out[...] = total

    for ref, n, sem in ((col_seg, n_row - 1, 0), (row_seg, chips - 1, 1), (row_land, chips - 1, 4), (col_land, n_row - 1, 5)):
        gone = ref.at[pl.ds(0, n * pb)]
        pltpu.make_async_copy(gone, gone, sent.at[sem]).wait()


def shards(amplitudes, energies, kernels, coefficients, target_block, source_block, slot_count):
    pb, states = amplitudes.shape
    n_row = lax.axis_size("row")
    n_col = lax.axis_size("col")
    nk, cap = coefficients.shape[2:4]
    n_src, n_tgt = n_col * pb, n_row * pb
    vmem = pl.BlockSpec(memory_space=pltpu.VMEM)
    hbm = pl.BlockSpec(memory_space=pl.ANY)
    dma = pltpu.SemaphoreType.DMA
    total = pl.pallas_call(
        functools.partial(body, n_row, n_col),
        out_shape=jax.ShapeDtypeStruct((pb, states), f32),
        in_specs=[vmem, hbm, hbm, vmem, vmem, pl.BlockSpec(memory_space=pltpu.SMEM)],
        out_specs=vmem,
        scratch_shapes=[
            pltpu.VMEM((nk, cap, states), bf16),
            pltpu.VMEM((nk, states, states), bf16),
            pltpu.VMEM((n_src, states), bf16),
            pltpu.VMEM((n_tgt, states), bf16),
            pltpu.VMEM((n_src, states), f32),
            pltpu.VMEM((n_tgt, states), f32),
            pltpu.VMEM((n_src // 2, states), f32),
            pltpu.VMEM((n_src // 2, states + LANES), i16),
            pltpu.VMEM((n_src // 2, states + LANES), i16),
            pltpu.VMEM((n_tgt, states + LANES), i16),
            pltpu.VMEM((n_tgt, states + LANES), i16),
            pltpu.VMEM((nk, cap, n_tgt), bf16),
            pltpu.VMEM((nk, n_src, cap), bf16),
            pltpu.VMEM((nk, cap, n_src), bf16),
            pltpu.VMEM((nk, n_tgt, cap), bf16),
            pltpu.VMEM((cap, states), bf16),
            pltpu.VMEM((cap, states), bf16),
            pltpu.VMEM((cap, states), bf16),
            pltpu.VMEM((cap, states), bf16),
            dma((2, nk)), dma, dma, dma, dma, dma, dma, dma((6,)),
        ],
        compiler_params=pltpu.CompilerParams(
            collective_id=0, has_side_effects=True, vmem_limit_bytes=60 * 1024 * 1024),
        name="couplings",
    )(amplitudes, coefficients.reshape(nk, cap, states), kernels,
      target_block.reshape(nk * cap // LANES, LANES), source_block.reshape(nk * cap // LANES, LANES),
      slot_count.reshape(nk))
    return total + energies * amplitudes.astype(f32)


def solution(mesh):
    in_specs = (
        P(("row", "col"), None),
        P(("row", "col"), None),
        P(),
        P("row", "col", None, None, None),
        P("row", "col", None, None),
        P("row", "col", None, None),
        P("row", "col", None),
    )
    out_specs = P(("row", "col"), None)
    return jax.shard_map(shards, mesh=mesh, in_specs=in_specs, out_specs=out_specs, check_vma=False)
```

```python
import functools
import jax
import jax.numpy as jnp
from jax import lax
from jax.experimental import pallas as pl
from jax.experimental.pallas import tpu as pltpu
from jax.sharding import PartitionSpec as P

MESH = pl.DeviceIdType.MESH
f32, bf16, i32, i16, f8 = jnp.float32, jnp.bfloat16, jnp.int32, jnp.int16, jnp.float8_e5m2
LANES = 128


def split(x):
    hi = x.astype(bf16)
    return hi, (x - hi.astype(f32)).astype(bf16)


def dot(a, b):
    return jnp.dot(a, b, preferred_element_type=f32)


def level(x):
    top = jnp.max(jnp.max(jnp.abs(x.astype(f32)), axis=0, keepdims=True), axis=1, keepdims=True)
    top = jnp.maximum(jnp.broadcast_to(top, (1, x.shape[1])), 1e-30)
    return jnp.ceil(jnp.log2(top * 0.125))


def encode(x):
    states = x.shape[1]
    top = jnp.maximum(jnp.max(jnp.abs(x), axis=1, keepdims=True), 1e-30)
    power = jnp.ceil(jnp.log2(jnp.broadcast_to(top, (x.shape[0], LANES)) * (1.0 / 32000.0)))
    scale = jnp.exp2(-power)
    parts = [jnp.round(x[:, at:at + LANES] * scale).astype(i32).astype(i16) for at in range(0, states, LANES)]
    return jnp.concatenate(parts + [power.astype(i32).astype(i16)], axis=1)


def decode(coded):
    states = coded.shape[1] - LANES
    scale = jnp.exp2(coded[:, states:].astype(i32).astype(f32))
    parts = [coded[:, at:at + LANES].astype(i32).astype(f32) * scale for at in range(0, states, LANES)]
    return jnp.concatenate(parts, axis=1)


def build(idx, cnt, k, rows_ref, cols_ref, count, rows8_ref=None):
    one, zero = jnp.bfloat16(1), jnp.bfloat16(0)
    for m in range(idx.shape[0]):
        lane = lax.broadcasted_iota(i32, (1, LANES), 1) + m * LANES
        row = jnp.where(lane < cnt[k], idx[m:m + 1, :], -1)
        wide = jnp.broadcast_to(row, (LANES, LANES))
        down, across = wide.astype(i16), wide.T.astype(i16)
        for base in range(0, count, LANES):
            it = lax.broadcasted_iota(i16, (LANES, LANES), 0)
            hot = jnp.where(it == down - jnp.int16(base), one, zero)
            rows_ref[k, pl.ds(base, LANES), pl.ds(m * LANES, LANES)] = hot
            if rows8_ref is not None:
                rows8_ref[k, pl.ds(base, LANES), pl.ds(m * LANES, LANES)] = hot.astype(f8)
            it = lax.broadcasted_iota(i16, (LANES, LANES), 1)
            cols_ref[k, pl.ds(m * LANES, LANES), pl.ds(base, LANES)] = jnp.where(it == across - jnp.int16(base), one, zero)


def zip_run(*gens):
    gens = list(gens)
    while gens:
        for g in list(gens):
            try:
                next(g)
            except StopIteration:
                gens.remove(g)


def body(n_row, n_col, amp, coef, kern, tgt_hbm, src_hbm, cnt, out,
         coef_v, kern_v, row_seg, col_seg, row_part, col_part, sibling_part,
         row_code, row_land, col_code, col_land,
         t_pick, t_put, t_put8, f_pick, f_put, hi_a, lo_a, lo8_a, hi_b, lo_b, lo8_b,
         kern_t, tab_a, tab_b, tgt, src,
         load_sem, index_sem, gather_row, gather_half, gather_col, cross, reduce_row, reduce_col, sent):
    r = lax.axis_index("row")
    c = lax.axis_index("col")
    core = lax.rem(c, 2)
    chip = lax.div(c, 2)
    chips = n_col // 2
    nk, cap, states = coef_v.shape
    pb = amp.shape[0]
    n_src, n_tgt = n_col * pb, n_row * pb
    half = n_src // 2
    groups = cap // LANES
    sibling = {"col": c + 1 - 2 * core}

    def piece(at):
        return pl.ds(pl.multiple_of(at * pb, pb), pb)

    mine, other = pl.ds(0, half), pl.ds(half, half)

    def load(k):
        return (pltpu.make_async_copy(kern.at[k], kern_v.at[k], load_sem.at[0, k]),
                pltpu.make_async_copy(coef.at[k], coef_v.at[k], load_sem.at[1, k]))

    def chip_peer(d):
        return lax.rem(chip + d, chips)

    def row_peer(d):
        return lax.rem(r + d, n_row)

    barrier = pltpu.get_barrier_semaphore()

    def greet_row(d, z):
        pl.semaphore_signal(barrier, inc=1, device_id={"row": row_peer(d)}, device_id_type=MESH)
        return z

    def greet_chip(d, z):
        pl.semaphore_signal(barrier, inc=1, device_id={"col": chip_peer(d) * 2 + core}, device_id_type=MESH)
        return z

    lax.fori_loop(1, n_row, greet_row, 0)
    lax.fori_loop(1, chips, greet_chip, 0)
    pl.semaphore_signal(barrier, inc=1, device_id=sibling, device_id_type=MESH)

    indices = (pltpu.make_async_copy(tgt_hbm, tgt, index_sem.at[0]),
               pltpu.make_async_copy(src_hbm, src, index_sem.at[1]))
    for copy in indices:
        copy.start()
    for k in range(nk):
        for copy in load(k):
            copy.start()
    own_row = pltpu.make_async_copy(amp, row_seg.at[piece(chip)], gather_row)
    own_col = pltpu.make_async_copy(amp, col_seg.at[piece(r)], gather_col)
    own_col.start()
    own_row.start()

    pl.semaphore_wait(barrier, n_row + chips - 1)

    def send_col_amp(d, z):
        pltpu.make_async_remote_copy(
            src_ref=amp, dst_ref=col_seg.at[piece(r)], send_sem=sent.at[0], recv_sem=gather_col,
            device_id={"row": row_peer(d)}, device_id_type=MESH).start()
        return z

    def send_row_amp(d, z):
        pltpu.make_async_remote_copy(
            src_ref=amp, dst_ref=row_seg.at[piece(chip)], send_sem=sent.at[1], recv_sem=gather_row,
            device_id={"col": chip_peer(d) * 2 + core}, device_id_type=MESH).start()
        return z

    lax.fori_loop(1, n_row, send_col_amp, 0)
    lax.fori_loop(1, chips, send_row_amp, 0)

    for copy in indices:
        copy.wait()

    def build_both(k, z):
        at = pl.ds(pl.multiple_of(k * groups, groups), groups)
        build(tgt[at, :], cnt, k, f_put, t_pick, n_tgt)
        j = src[at, :]
        piece_of = lax.shift_right_logical(j, 4)
        spot = ((piece_of & 1) ^ core) * half + lax.shift_right_logical(piece_of, 1) * pb + (j & (pb - 1))
        build(spot, cnt, k, t_put, f_pick, n_src, t_put8)
        return z

    lax.fori_loop(0, nk, build_both, 0)
    row_part[...] = jnp.zeros_like(row_part)
    col_part[...] = jnp.zeros_like(col_part)
    for k in range(nk):
        for copy in load(k):
            copy.wait()

    def turn(k, z):
        kern_t[k] = kern_v[k].T
        return z

    lax.fori_loop(0, nk, turn, 0)
    pltpu.make_async_copy(col_seg, col_seg, gather_col).wait()

    step = cap // 4
    t_level = level(col_seg[...])
    t_up, t_down = jnp.exp2(14.0 - t_level), jnp.exp2(t_level - 14.0)

    def t_table(k, tab):
        h, l = split(dot(col_seg[...], kern_t[k]))
        tab[pl.ds(0, n_tgt), :] = h
        tab[pl.ds(n_tgt, n_tgt), :] = l
        yield

    def t_prep(k, tab, hi, lo8):
        both = tab[...]
        for at in range(0, cap, step):
            p = t_pick[k, pl.ds(at, step), :]
            val = dot(jnp.concatenate([p, p], axis=1), both) * coef_v[k, pl.ds(at, step), :].astype(f32)
            h = val.astype(bf16)
            hi[pl.ds(at, step), :] = h
            lo8[pl.ds(at, step), :] = ((val - h.astype(f32)) * t_up).astype(f8)
            yield

    def t_fill(k, hi, lo8, rows):
        for at in range(0, states, 256):
            lanes = pl.ds(at, 256)
            row_part[rows, lanes] += (dot(t_put[k, rows, :], hi[:, lanes])
                                      + dot(t_put8[k, rows, :], lo8[:, lanes]) * t_down[:, at:at + 256])
            yield

    def f_prep(k, hi, lo):
        for at in range(0, cap, step):
            val = dot(f_pick[k, pl.ds(at, step), :], row_seg[...]) * coef_v[k, pl.ds(at, step), :].astype(f32)
            hi[pl.ds(at, step), :], lo[pl.ds(at, step), :] = split(val)
            yield

    def f_fill(k, hi, lo):
        p = f_put[k]
        parts = []
        for at in range(0, states, 256):
            lanes = pl.ds(at, 256)
            parts.append(jnp.concatenate(split(dot(p, hi[:, lanes]) + dot(p, lo[:, lanes])), axis=0))
            yield
        both = jnp.concatenate(parts, axis=1)
        for at in range(0, states, 256):
            lanes = pl.ds(at, 256)
            wide = dot(both, kern_v[k, :, lanes])
            col_part[:, lanes] += wide[:n_tgt] + wide[n_tgt:]
            yield

    t_bufs = [(hi_a, lo8_a), (hi_b, lo8_b)]
    bufs = [(hi_a, lo_a), (hi_b, lo_b)]
    tabs = [tab_a, tab_b]
    every = pl.ds(0, n_src)
    hand = pltpu.make_async_remote_copy(
        src_ref=row_seg.at[mine], dst_ref=row_seg.at[other], send_sem=sent.at[2], recv_sem=gather_half,
        device_id=sibling, device_id_type=MESH)

    zip_run(t_table(0, tab_a))
    zip_run(t_prep(0, tab_a, *t_bufs[0]), t_table(1, tab_b))
    for k in range(nk - 1):
        todo = [t_fill(k, *t_bufs[k % 2], every), t_prep(k + 1, tabs[(k + 1) % 2], *t_bufs[(k + 1) % 2])]
        if k + 2 < nk:
            todo.append(t_table(k + 2, tabs[k % 2]))
        zip_run(*todo)
        if k == 1:
            pltpu.make_async_copy(row_seg.at[mine], row_seg.at[mine], gather_row).wait()
            hand.start()
    hand.wait()
    last = t_bufs[(nk - 1) % 2]
    first = f_prep(0, *bufs[nk % 2])
    for done in t_fill(nk - 1, *last, other):
        next(first)

    swap = pltpu.make_async_remote_copy(
        src_ref=row_part.at[other], dst_ref=sibling_part, send_sem=sent.at[3], recv_sem=cross,
        device_id=sibling, device_id_type=MESH)
    swap.start()

    zip_run(t_fill(nk - 1, *last, mine), first)

    zip_run(f_fill(0, *bufs[nk % 2]), f_prep(1, *bufs[(nk + 1) % 2]))

    swap.wait()

    def code_row(i, z):
        at = pl.ds(pl.multiple_of(i * 64, 64), 64)
        total = row_part[at, :] + sibling_part[at, :]
        row_code[at, :] = encode(total)
        return z

    lax.fori_loop(0, half // 64, code_row, 0)

    def send_row(d, z):
        peer = chip_peer(d)
        pltpu.make_async_remote_copy(
            src_ref=row_code.at[piece(peer)], dst_ref=row_land.at[piece(chip)],
            send_sem=sent.at[4], recv_sem=reduce_row,
            device_id={"col": peer * 2 + core}, device_id_type=MESH).start()
        return z

    lax.fori_loop(1, chips, send_row, 0)
    own = pltpu.make_async_copy(row_code.at[piece(chip)], row_land.at[piece(chip)], reduce_row)
    own.start()

    for k in range(1, nk - 1):
        zip_run(f_fill(k, *bufs[(nk + k) % 2]), f_prep(k + 1, *bufs[(nk + k + 1) % 2]))
    zip_run(f_fill(nk - 1, *bufs[(2 * nk - 1) % 2]))

    col_code[...] = encode(col_part[...])

    def send_col(d, z):
        peer = row_peer(d)
        pltpu.make_async_remote_copy(
            src_ref=col_code.at[piece(peer)], dst_ref=col_land.at[piece(r)],
            send_sem=sent.at[5], recv_sem=reduce_col,
            device_id={"row": peer}, device_id_type=MESH).start()
        return z

    lax.fori_loop(1, n_row, send_col, 0)
    own = pltpu.make_async_copy(col_code.at[piece(r)], col_land.at[piece(r)], reduce_col)
    own.start()

    pltpu.make_async_copy(row_land, row_land, reduce_row).wait()
    total = decode(row_land[pl.ds(0, pb), :])
    for j in range(1, chips):
        total = total + decode(row_land[pl.ds(j * pb, pb), :])
    pltpu.make_async_copy(col_land, col_land, reduce_col).wait()
    for j in range(n_row):
        total = total + decode(col_land[pl.ds(j * pb, pb), :])
    out[...] = total

    for ref, n, sem in ((col_seg, n_row - 1, 0), (row_seg, chips - 1, 1), (row_land, chips - 1, 4), (col_land, n_row - 1, 5)):
        gone = ref.at[pl.ds(0, n * pb)]
        pltpu.make_async_copy(gone, gone, sent.at[sem]).wait()


def shards(amplitudes, energies, kernels, coefficients, target_block, source_block, slot_count):
    pb, states = amplitudes.shape
    n_row = lax.axis_size("row")
    n_col = lax.axis_size("col")
    nk, cap = coefficients.shape[2:4]
    n_src, n_tgt = n_col * pb, n_row * pb
    vmem = pl.BlockSpec(memory_space=pltpu.VMEM)
    hbm = pl.BlockSpec(memory_space=pl.ANY)
    dma = pltpu.SemaphoreType.DMA
    total = pl.pallas_call(
        functools.partial(body, n_row, n_col),
        out_shape=jax.ShapeDtypeStruct((pb, states), f32),
        in_specs=[hbm, hbm, hbm, hbm, hbm, pl.BlockSpec(memory_space=pltpu.SMEM)],
        out_specs=vmem,
        scratch_shapes=[
            pltpu.VMEM((nk, cap, states), bf16),
            pltpu.VMEM((nk, states, states), bf16),
            pltpu.VMEM((n_src, states), bf16),
            pltpu.VMEM((n_tgt, states), bf16),
            pltpu.VMEM((n_src, states), f32),
            pltpu.VMEM((n_tgt, states), f32),
            pltpu.VMEM((n_src // 2, states), f32),
            pltpu.VMEM((n_src // 2, states + LANES), i16),
            pltpu.VMEM((n_src // 2, states + LANES), i16),
            pltpu.VMEM((n_tgt, states + LANES), i16),
            pltpu.VMEM((n_tgt, states + LANES), i16),
            pltpu.VMEM((nk, cap, n_tgt), bf16),
            pltpu.VMEM((nk, n_src, cap), bf16),
            pltpu.VMEM((nk, n_src, cap), f8),
            pltpu.VMEM((nk, cap, n_src), bf16),
            pltpu.VMEM((nk, n_tgt, cap), bf16),
            pltpu.VMEM((cap, states), bf16),
            pltpu.VMEM((cap, states), bf16),
            pltpu.VMEM((cap, states), f8),
            pltpu.VMEM((cap, states), bf16),
            pltpu.VMEM((cap, states), bf16),
            pltpu.VMEM((cap, states), f8),
            pltpu.VMEM((nk, states, states), bf16),
            pltpu.VMEM((2 * n_tgt, states), bf16),
            pltpu.VMEM((2 * n_tgt, states), bf16),
            pltpu.VMEM((nk * cap // LANES, LANES), i32),
            pltpu.VMEM((nk * cap // LANES, LANES), i32),
            dma((2, nk)), dma((2,)), dma, dma, dma, dma, dma, dma, dma((6,)),
        ],
        compiler_params=pltpu.CompilerParams(
            collective_id=0, has_side_effects=True, vmem_limit_bytes=60 * 1024 * 1024),
        name="couplings",
    )(amplitudes, coefficients.reshape(nk, cap, states), kernels,
      target_block.reshape(nk * cap // LANES, LANES), source_block.reshape(nk * cap // LANES, LANES),
      slot_count.reshape(nk))
    return total + energies * amplitudes.astype(f32)


def solution(mesh):
    in_specs = (
        P(("row", "col"), None),
        P(("row", "col"), None),
        P(),
        P("row", "col", None, None, None),
        P("row", "col", None, None),
        P("row", "col", None, None),
        P("row", "col", None),
    )
    out_specs = P(("row", "col"), None)
    return jax.shard_map(shards, mesh=mesh, in_specs=in_specs, out_specs=out_specs, check_vma=False)
```

```python
import functools
import jax
import jax.numpy as jnp
from jax import lax
from jax.experimental import pallas as pl
from jax.experimental.pallas import tpu as pltpu
from jax.sharding import PartitionSpec as P

MESH = pl.DeviceIdType.MESH
f32, bf16, i32, i16, f8 = jnp.float32, jnp.bfloat16, jnp.int32, jnp.int16, jnp.float8_e5m2
LANES = 128


def split(x):
    hi = x.astype(bf16)
    return hi, (x - hi.astype(f32)).astype(bf16)


def dot(a, b):
    return jnp.dot(a, b, preferred_element_type=f32)


def level(x):
    top = jnp.max(jnp.max(jnp.abs(x.astype(f32)), axis=0, keepdims=True), axis=1, keepdims=True)
    top = jnp.maximum(jnp.broadcast_to(top, (1, x.shape[1])), 1e-30)
    return jnp.ceil(jnp.log2(top * 0.125))


def encode(x):
    states = x.shape[1]
    top = jnp.maximum(jnp.max(jnp.abs(x), axis=1, keepdims=True), 1e-30)
    power = jnp.ceil(jnp.log2(jnp.broadcast_to(top, (x.shape[0], LANES)) * (1.0 / 32000.0)))
    scale = jnp.exp2(-power)
    parts = [jnp.round(x[:, at:at + LANES] * scale).astype(i32).astype(i16) for at in range(0, states, LANES)]
    return jnp.concatenate(parts + [power.astype(i32).astype(i16)], axis=1)


def decode(coded):
    states = coded.shape[1] - LANES
    scale = jnp.exp2(coded[:, states:].astype(i32).astype(f32))
    parts = [coded[:, at:at + LANES].astype(i32).astype(f32) * scale for at in range(0, states, LANES)]
    return jnp.concatenate(parts, axis=1)


def build(idx, cnt, k, rows_ref, cols_ref, count, rows8_ref=None):
    one, zero = jnp.bfloat16(1), jnp.bfloat16(0)
    for m in range(idx.shape[0]):
        lane = lax.broadcasted_iota(i32, (1, LANES), 1) + m * LANES
        row = jnp.where(lane < cnt[k], idx[m:m + 1, :], -1)
        wide = jnp.broadcast_to(row, (LANES, LANES))
        down, across = wide.astype(i16), wide.T.astype(i16)
        for base in range(0, count, LANES):
            it = lax.broadcasted_iota(i16, (LANES, LANES), 0)
            hot = jnp.where(it == down - jnp.int16(base), one, zero)
            rows_ref[k, pl.ds(base, LANES), pl.ds(m * LANES, LANES)] = hot
            if rows8_ref is not None:
                rows8_ref[k, pl.ds(base, LANES), pl.ds(m * LANES, LANES)] = hot.astype(f8)
            it = lax.broadcasted_iota(i16, (LANES, LANES), 1)
            cols_ref[k, pl.ds(m * LANES, LANES), pl.ds(base, LANES)] = jnp.where(it == across - jnp.int16(base), one, zero)


def zip_run(*gens):
    gens = list(gens)
    while gens:
        for g in list(gens):
            try:
                next(g)
            except StopIteration:
                gens.remove(g)


def body(n_row, n_col, amp, coef, kern, tgt_hbm, src_hbm, cnt, out,
         coef_v, kern_v, row_seg, col_seg, row_part, col_part, sibling_part,
         row_code, row_land, col_code, col_land,
         t_pick, t_put, t_put8, f_pick, f_put, hi_a, lo_a, lo8_a, hi_b, lo_b, lo8_b,
         kern_t, tab_a, tab_b, tgt, src,
         load_sem, index_sem, gather_row, gather_half, gather_col, cross, reduce_row, reduce_col, sent):
    r = lax.axis_index("row")
    c = lax.axis_index("col")
    core = lax.rem(c, 2)
    chip = lax.div(c, 2)
    chips = n_col // 2
    nk, cap, states = coef_v.shape
    pb = amp.shape[0]
    n_src, n_tgt = n_col * pb, n_row * pb
    half = n_src // 2
    groups = cap // LANES
    sibling = {"col": c + 1 - 2 * core}

    def piece(at):
        return pl.ds(pl.multiple_of(at * pb, pb), pb)

    mine, other = pl.ds(0, half), pl.ds(half, half)

    def load(k):
        return (pltpu.make_async_copy(kern.at[k], kern_v.at[k], load_sem.at[0, k]),
                pltpu.make_async_copy(coef.at[k], coef_v.at[k], load_sem.at[1, k]))

    def chip_peer(d):
        return lax.rem(chip + d, chips)

    def row_peer(d):
        return lax.rem(r + d, n_row)

    barrier = pltpu.get_barrier_semaphore()

    def greet_row(d, z):
        pl.semaphore_signal(barrier, inc=1, device_id={"row": row_peer(d)}, device_id_type=MESH)
        return z

    def greet_chip(d, z):
        pl.semaphore_signal(barrier, inc=1, device_id={"col": chip_peer(d) * 2 + core}, device_id_type=MESH)
        return z

    lax.fori_loop(1, n_row, greet_row, 0)
    lax.fori_loop(1, chips, greet_chip, 0)
    pl.semaphore_signal(barrier, inc=1, device_id=sibling, device_id_type=MESH)

    indices = (pltpu.make_async_copy(tgt_hbm, tgt, index_sem.at[0]),
               pltpu.make_async_copy(src_hbm, src, index_sem.at[1]))
    for copy in indices:
        copy.start()
    for k in range(nk):
        for copy in load(k):
            copy.start()
    own_row = pltpu.make_async_copy(amp, row_seg.at[piece(chip)], gather_row)
    own_col = pltpu.make_async_copy(amp, col_seg.at[piece(r)], gather_col)
    own_col.start()
    own_row.start()

    pl.semaphore_wait(barrier, n_row + chips - 1)

    def send_col_amp(d, z):
        pltpu.make_async_remote_copy(
            src_ref=amp, dst_ref=col_seg.at[piece(r)], send_sem=sent.at[0], recv_sem=gather_col,
            device_id={"row": row_peer(d)}, device_id_type=MESH).start()
        return z

    def send_row_amp(d, z):
        pltpu.make_async_remote_copy(
            src_ref=amp, dst_ref=row_seg.at[piece(chip)], send_sem=sent.at[1], recv_sem=gather_row,
            device_id={"col": chip_peer(d) * 2 + core}, device_id_type=MESH).start()
        return z

    lax.fori_loop(1, n_row, send_col_amp, 0)
    lax.fori_loop(1, chips, send_row_amp, 0)

    for copy in indices:
        copy.wait()

    def build_both(k, z):
        at = pl.ds(pl.multiple_of(k * groups, groups), groups)
        build(tgt[at, :], cnt, k, f_put, t_pick, n_tgt)
        j = src[at, :]
        piece_of = lax.shift_right_logical(j, 4)
        spot = ((piece_of & 1) ^ core) * half + lax.shift_right_logical(piece_of, 1) * pb + (j & (pb - 1))
        build(spot, cnt, k, t_put, f_pick, n_src, t_put8)
        return z

    lax.fori_loop(0, nk, build_both, 0)
    row_part[...] = jnp.zeros_like(row_part)
    col_part[...] = jnp.zeros_like(col_part)
    for k in range(nk):
        for copy in load(k):
            copy.wait()

    def turn(k, z):
        kern_t[k] = kern_v[k].T
        return z

    lax.fori_loop(0, nk, turn, 0)
    pltpu.make_async_copy(col_seg, col_seg, gather_col).wait()

    step = cap // 4
    t_level = level(col_seg[...])
    t_up, t_down = jnp.exp2(14.0 - t_level), jnp.exp2(t_level - 14.0)

    def t_table(k, tab):
        h, l = split(dot(col_seg[...], kern_t[k]))
        tab[pl.ds(0, n_tgt), :] = h
        tab[pl.ds(n_tgt, n_tgt), :] = l
        yield

    def t_prep(k, tab, hi, lo8):
        both = tab[...]
        for at in range(0, cap, step):
            p = t_pick[k, pl.ds(at, step), :]
            val = dot(jnp.concatenate([p, p], axis=1), both) * coef_v[k, pl.ds(at, step), :].astype(f32)
            h = val.astype(bf16)
            hi[pl.ds(at, step), :] = h
            lo8[pl.ds(at, step), :] = ((val - h.astype(f32)) * t_up).astype(f8)
            yield

    def t_fill(k, hi, lo8, rows):
        for at in range(0, states, 256):
            lanes = pl.ds(at, 256)
            row_part[rows, lanes] += (dot(t_put[k, rows, :], hi[:, lanes])
                                      + dot(t_put8[k, rows, :], lo8[:, lanes]) * t_down[:, at:at + 256])
            yield

    def f_prep(k, hi, lo):
        for at in range(0, cap, step):
            val = dot(f_pick[k, pl.ds(at, step), :], row_seg[...]) * coef_v[k, pl.ds(at, step), :].astype(f32)
            hi[pl.ds(at, step), :], lo[pl.ds(at, step), :] = split(val)
            yield

    def f_fill(k, hi, lo):
        p = f_put[k]
        parts = []
        for at in range(0, states, 256):
            lanes = pl.ds(at, 256)
            parts.append(jnp.concatenate(split(dot(p, hi[:, lanes]) + dot(p, lo[:, lanes])), axis=0))
            yield
        both = jnp.concatenate(parts, axis=1)
        for at in range(0, states, 256):
            lanes = pl.ds(at, 256)
            wide = dot(both, kern_v[k, :, lanes])
            col_part[:, lanes] += wide[:n_tgt] + wide[n_tgt:]
            yield

    t_bufs = [(hi_a, lo8_a), (hi_b, lo8_b)]
    bufs = [(hi_a, lo_a), (hi_b, lo_b)]
    tabs = [tab_a, tab_b]
    every = pl.ds(0, n_src)
    hand = pltpu.make_async_remote_copy(
        src_ref=row_seg.at[mine], dst_ref=row_seg.at[other], send_sem=sent.at[2], recv_sem=gather_half,
        device_id=sibling, device_id_type=MESH)

    zip_run(t_table(0, tab_a))
    zip_run(t_prep(0, tab_a, *t_bufs[0]), t_table(1, tab_b))
    for k in range(nk - 1):
        todo = [t_fill(k, *t_bufs[k % 2], every), t_prep(k + 1, tabs[(k + 1) % 2], *t_bufs[(k + 1) % 2])]
        if k + 2 < nk:
            todo.append(t_table(k + 2, tabs[k % 2]))
        zip_run(*todo)
        if k == 1:
            pltpu.make_async_copy(row_seg.at[mine], row_seg.at[mine], gather_row).wait()
            hand.start()
    hand.wait()
    last = t_bufs[(nk - 1) % 2]
    first = f_prep(0, *bufs[nk % 2])
    for done in t_fill(nk - 1, *last, other):
        next(first)

    swap = pltpu.make_async_remote_copy(
        src_ref=row_part.at[other], dst_ref=sibling_part, send_sem=sent.at[3], recv_sem=cross,
        device_id=sibling, device_id_type=MESH)
    swap.start()

    zip_run(t_fill(nk - 1, *last, mine), first)

    zip_run(f_fill(0, *bufs[nk % 2]), f_prep(1, *bufs[(nk + 1) % 2]))

    swap.wait()

    def code_row(i, z):
        at = pl.ds(pl.multiple_of(i * 64, 64), 64)
        total = row_part[at, :] + sibling_part[at, :]
        row_code[at, :] = encode(total)
        return z

    lax.fori_loop(0, half // 64, code_row, 0)

    def send_row(d, z):
        peer = chip_peer(d)
        pltpu.make_async_remote_copy(
            src_ref=row_code.at[piece(peer)], dst_ref=row_land.at[piece(chip)],
            send_sem=sent.at[4], recv_sem=reduce_row,
            device_id={"col": peer * 2 + core}, device_id_type=MESH).start()
        return z

    lax.fori_loop(1, chips, send_row, 0)
    own = pltpu.make_async_copy(row_code.at[piece(chip)], row_land.at[piece(chip)], reduce_row)
    own.start()

    for k in range(1, nk - 1):
        zip_run(f_fill(k, *bufs[(nk + k) % 2]), f_prep(k + 1, *bufs[(nk + k + 1) % 2]))
    zip_run(f_fill(nk - 1, *bufs[(2 * nk - 1) % 2]))

    col_code[...] = encode(col_part[...])

    def send_col(d, z):
        peer = row_peer(d)
        pltpu.make_async_remote_copy(
            src_ref=col_code.at[piece(peer)], dst_ref=col_land.at[piece(r)],
            send_sem=sent.at[5], recv_sem=reduce_col,
            device_id={"row": peer}, device_id_type=MESH).start()
        return z

    lax.fori_loop(1, n_row, send_col, 0)
    own = pltpu.make_async_copy(col_code.at[piece(r)], col_land.at[piece(r)], reduce_col)
    own.start()

    pltpu.make_async_copy(row_land, row_land, reduce_row).wait()
    total = decode(row_land[pl.ds(0, pb), :])
    for j in range(1, chips):
        total = total + decode(row_land[pl.ds(j * pb, pb), :])
    pltpu.make_async_copy(col_land, col_land, reduce_col).wait()
    for j in range(n_row):
        total = total + decode(col_land[pl.ds(j * pb, pb), :])
    out[...] = total

    for ref, n, sem in ((col_seg, n_row - 1, 0), (row_seg, chips - 1, 1), (row_land, chips - 1, 4), (col_land, n_row - 1, 5)):
        gone = ref.at[pl.ds(0, n * pb)]
        pltpu.make_async_copy(gone, gone, sent.at[sem]).wait()


def shards(amplitudes, energies, kernels, coefficients, target_block, source_block, slot_count):
    pb, states = amplitudes.shape
    n_row = lax.axis_size("row")
    n_col = lax.axis_size("col")
    nk, cap = coefficients.shape[2:4]
    n_src, n_tgt = n_col * pb, n_row * pb
    vmem = pl.BlockSpec(memory_space=pltpu.VMEM)
    hbm = pl.BlockSpec(memory_space=pl.ANY)
    dma = pltpu.SemaphoreType.DMA
    total = pl.pallas_call(
        functools.partial(body, n_row, n_col),
        out_shape=pltpu.VMEM((pb, states), f32),
        in_specs=[hbm, hbm, hbm, hbm, hbm, pl.BlockSpec(memory_space=pltpu.SMEM)],
        out_specs=vmem,
        scratch_shapes=[
            pltpu.VMEM((nk, cap, states), bf16),
            pltpu.VMEM((nk, states, states), bf16),
            pltpu.VMEM((n_src, states), bf16),
            pltpu.VMEM((n_tgt, states), bf16),
            pltpu.VMEM((n_src, states), f32),
            pltpu.VMEM((n_tgt, states), f32),
            pltpu.VMEM((n_src // 2, states), f32),
            pltpu.VMEM((n_src // 2, states + LANES), i16),
            pltpu.VMEM((n_src // 2, states + LANES), i16),
            pltpu.VMEM((n_tgt, states + LANES), i16),
            pltpu.VMEM((n_tgt, states + LANES), i16),
            pltpu.VMEM((nk, cap, n_tgt), bf16),
            pltpu.VMEM((nk, n_src, cap), bf16),
            pltpu.VMEM((nk, n_src, cap), f8),
            pltpu.VMEM((nk, cap, n_src), bf16),
            pltpu.VMEM((nk, n_tgt, cap), bf16),
            pltpu.VMEM((cap, states), bf16),
            pltpu.VMEM((cap, states), bf16),
            pltpu.VMEM((cap, states), f8),
            pltpu.VMEM((cap, states), bf16),
            pltpu.VMEM((cap, states), bf16),
            pltpu.VMEM((cap, states), f8),
            pltpu.VMEM((nk, states, states), bf16),
            pltpu.VMEM((2 * n_tgt, states), bf16),
            pltpu.VMEM((2 * n_tgt, states), bf16),
            pltpu.VMEM((nk * cap // LANES, LANES), i32),
            pltpu.VMEM((nk * cap // LANES, LANES), i32),
            dma((2, nk)), dma((2,)), dma, dma, dma, dma, dma, dma, dma((6,)),
        ],
        compiler_params=pltpu.CompilerParams(
            collective_id=0, has_side_effects=True, vmem_limit_bytes=60 * 1024 * 1024),
        name="couplings",
    )(amplitudes, coefficients.reshape(nk, cap, states), kernels,
      target_block.reshape(nk * cap // LANES, LANES), source_block.reshape(nk * cap // LANES, LANES),
      slot_count.reshape(nk))
    return total + energies * amplitudes.astype(f32)


def solution(mesh):
    in_specs = (
        P(("row", "col"), None),
        P(("row", "col"), None),
        P(),
        P("row", "col", None, None, None),
        P("row", "col", None, None),
        P("row", "col", None, None),
        P("row", "col", None),
    )
    out_specs = P(("row", "col"), None)
    return jax.shard_map(shards, mesh=mesh, in_specs=in_specs, out_specs=out_specs, check_vma=False)
```

```python
import functools
import jax
import jax.numpy as jnp
from jax import lax
from jax.experimental import pallas as pl
from jax.experimental.pallas import tpu as pltpu
from jax.sharding import PartitionSpec as P

MESH = pl.DeviceIdType.MESH
f32, bf16, i32, i16, f8 = jnp.float32, jnp.bfloat16, jnp.int32, jnp.int16, jnp.float8_e5m2
LANES = 128
LINE = 4


def split(x):
    hi = x.astype(bf16)
    return hi, (x - hi.astype(f32)).astype(bf16)


def dot(a, b):
    return jnp.dot(a, b, preferred_element_type=f32)


def level(x):
    top = jnp.max(jnp.max(jnp.abs(x.astype(f32)), axis=0, keepdims=True), axis=1, keepdims=True)
    top = jnp.maximum(jnp.broadcast_to(top, (1, x.shape[1])), 1e-30)
    return jnp.ceil(jnp.log2(top * 0.125))


def encode(x):
    states = x.shape[1]
    top = jnp.maximum(jnp.max(jnp.abs(x), axis=1, keepdims=True), 1e-30)
    power = jnp.ceil(jnp.log2(jnp.broadcast_to(top, (x.shape[0], LANES)) * (1.0 / 32000.0)))
    scale = jnp.exp2(-power)
    parts = [jnp.round(x[:, at:at + LANES] * scale).astype(i32).astype(i16) for at in range(0, states, LANES)]
    return jnp.concatenate(parts + [power.astype(i32).astype(i16)], axis=1)


def decode(coded):
    states = coded.shape[1] - LANES
    scale = jnp.exp2(coded[:, states:].astype(i32).astype(f32))
    parts = [coded[:, at:at + LANES].astype(i32).astype(f32) * scale for at in range(0, states, LANES)]
    return jnp.concatenate(parts, axis=1)


def build(idx, cnt, k, rows_ref, cols_ref, count, rows8_ref=None):
    one, zero = jnp.bfloat16(1), jnp.bfloat16(0)
    for m in range(idx.shape[0]):
        lane = lax.broadcasted_iota(i32, (1, LANES), 1) + m * LANES
        row = jnp.where(lane < cnt[k], idx[m:m + 1, :], -1)
        wide = jnp.broadcast_to(row, (LANES, LANES))
        down, across = wide.astype(i16), wide.T.astype(i16)
        for base in range(0, count, LANES):
            it = lax.broadcasted_iota(i16, (LANES, LANES), 0)
            hot = jnp.where(it == down - jnp.int16(base), one, zero)
            rows_ref[k, pl.ds(base, LANES), pl.ds(m * LANES, LANES)] = hot
            if rows8_ref is not None:
                rows8_ref[k, pl.ds(base, LANES), pl.ds(m * LANES, LANES)] = hot.astype(f8)
            it = lax.broadcasted_iota(i16, (LANES, LANES), 1)
            cols_ref[k, pl.ds(m * LANES, LANES), pl.ds(base, LANES)] = jnp.where(it == across - jnp.int16(base), one, zero)


def zip_run(*gens):
    gens = list(gens)
    while gens:
        for g in list(gens):
            try:
                next(g)
            except StopIteration:
                gens.remove(g)


def body(n_row, n_col, amp, coef, kern, tgt_hbm, src_hbm, cnt, out,
         coef_v, kern_v, row_seg, col_seg, row_part, col_part, sibling_part,
         row_code, row_land, near_code, near_land, col_code, col_land,
         t_pick, t_put, t_put8, f_pick, f_put, t_hi, t_lo8, hi_a, lo_a, hi_b, lo_b,
         kern_t, tab_a, tab_b, tgt, src,
         load_sem, index_sem, gather_row, gather_half, gather_col, cross, reduce_row, reduce_near, reduce_col, sent):
    r = lax.axis_index("row")
    c = lax.axis_index("col")
    core = lax.rem(c, 2)
    chip = lax.div(c, 2)
    chips = n_col // 2
    nk, cap, states = coef_v.shape
    pb = amp.shape[0]
    n_src, n_tgt = n_col * pb, n_row * pb
    lines = chips // LINE
    line, at_x = lax.div(chip, LINE), lax.rem(chip, LINE)
    near = 2 * LINE * pb
    far = (chips - LINE) * pb
    near_mine, near_other = pl.ds(0, near // 2), pl.ds(near // 2, near // 2)
    far_mine, far_other = pl.ds(near, far), pl.ds(near + far, far)
    near_rows = pl.ds(0, near)
    groups = cap // LANES
    sibling = {"col": c + 1 - 2 * core}

    def piece(at):
        return pl.ds(pl.multiple_of(at * pb, pb), pb)

    def load(k):
        return (pltpu.make_async_copy(kern.at[k], kern_v.at[k], load_sem.at[0, k]),
                pltpu.make_async_copy(coef.at[k], coef_v.at[k], load_sem.at[1, k]))

    def chip_peer(d):
        return lax.rem(chip + d, chips)

    def row_peer(d):
        return lax.rem(r + d, n_row)

    def line_col(x, q):
        return (line * LINE + x) * 2 + q

    def far_peer(t):
        ahead = lax.div(t, LINE) + 1
        there = lax.rem(line + ahead, lines)
        return (there * LINE + lax.rem(t, LINE)) * 2 + core, (lines - ahead - 1) * LINE + at_x

    barrier = pltpu.get_barrier_semaphore()

    def greet_row(d, z):
        pl.semaphore_signal(barrier, inc=1, device_id={"row": row_peer(d)}, device_id_type=MESH)
        return z

    def greet_chip(d, z):
        pl.semaphore_signal(barrier, inc=1, device_id={"col": chip_peer(d) * 2 + core}, device_id_type=MESH)
        return z

    lax.fori_loop(1, n_row, greet_row, 0)
    lax.fori_loop(1, chips, greet_chip, 0)

    def greet_line(x, z):
        pl.semaphore_signal(barrier, inc=1, device_id={"col": line_col(x, 1 - core)}, device_id_type=MESH)
        return z

    lax.fori_loop(0, LINE, greet_line, 0)

    indices = (pltpu.make_async_copy(tgt_hbm, tgt, index_sem.at[0]),
               pltpu.make_async_copy(src_hbm, src, index_sem.at[1]))
    for copy in indices:
        copy.start()
    for k in range(nk):
        for copy in load(k):
            copy.start()
    own_row = pltpu.make_async_copy(amp, row_seg.at[piece(at_x)], gather_row.at[0])
    own_col = pltpu.make_async_copy(amp, col_seg.at[piece(r)], gather_col)
    own_col.start()
    own_row.start()

    pl.semaphore_wait(barrier, n_row + chips + LINE - 2)

    def send_col_amp(d, z):
        pltpu.make_async_remote_copy(
            src_ref=amp, dst_ref=col_seg.at[piece(r)], send_sem=sent.at[0], recv_sem=gather_col,
            device_id={"row": row_peer(d)}, device_id_type=MESH).start()
        return z

    def send_near_amp(d, z):
        pltpu.make_async_remote_copy(
            src_ref=amp, dst_ref=row_seg.at[piece(at_x)], send_sem=sent.at[1], recv_sem=gather_row.at[0],
            device_id={"col": line_col(lax.rem(at_x + d, LINE), core)}, device_id_type=MESH).start()
        return z

    def send_far_amp(t, z):
        peer, spot = far_peer(t)
        pltpu.make_async_remote_copy(
            src_ref=amp, dst_ref=row_seg.at[piece(2 * LINE + spot)], send_sem=sent.at[1], recv_sem=gather_row.at[1],
            device_id={"col": peer}, device_id_type=MESH).start()
        return z

    lax.fori_loop(1, n_row, send_col_amp, 0)
    lax.fori_loop(1, LINE, send_near_amp, 0)
    lax.fori_loop(0, chips - LINE, send_far_amp, 0)

    for copy in indices:
        copy.wait()

    def build_both(k, z):
        at = pl.ds(pl.multiple_of(k * groups, groups), groups)
        build(tgt[at, :], cnt, k, f_put, t_pick, n_tgt)
        j = src[at, :]
        piece_of = lax.shift_right_logical(j, 4)
        swapped = (piece_of & 1) ^ core
        of_line = lax.shift_right_logical(piece_of, 1)
        ahead = (lax.shift_right_logical(of_line, 2) - line + lines) & (lines - 1)
        x = of_line & (LINE - 1)
        spot = jnp.where(ahead == 0, swapped * (near // 2) + x * pb,
                         near + swapped * far + ((ahead - 1) * LINE + x) * pb) + (j & (pb - 1))
        build(spot, cnt, k, t_put, f_pick, n_src, t_put8)
        return z

    lax.fori_loop(0, nk, build_both, 0)
    row_part[...] = jnp.zeros_like(row_part)
    col_part[...] = jnp.zeros_like(col_part)
    for k in range(nk):
        for copy in load(k):
            copy.wait()

    def turn(k, z):
        kern_t[k] = kern_v[k].T
        return z

    lax.fori_loop(0, nk, turn, 0)
    pltpu.make_async_copy(col_seg, col_seg, gather_col).wait()

    step = cap // 4
    t_level = level(col_seg[...])
    t_up, t_down = jnp.exp2(14.0 - t_level), jnp.exp2(t_level - 14.0)

    def t_table(k, tab):
        h, l = split(dot(col_seg[...], kern_t[k]))
        tab[pl.ds(0, n_tgt), :] = h
        tab[pl.ds(n_tgt, n_tgt), :] = l
        yield

    def t_prep(k, tab):
        both = tab[...]
        for at in range(0, cap, step):
            p = t_pick[k, pl.ds(at, step), :]
            val = dot(jnp.concatenate([p, p], axis=1), both) * coef_v[k, pl.ds(at, step), :].astype(f32)
            h = val.astype(bf16)
            t_hi[k, pl.ds(at, step), :] = h
            t_lo8[k, pl.ds(at, step), :] = ((val - h.astype(f32)) * t_up).astype(f8)
            yield

    def t_fill(k, rows):
        for at in range(0, states, 256):
            lanes = pl.ds(at, 256)
            row_part[rows, lanes] += (dot(t_put[k, rows, :], t_hi[k, :, lanes])
                                      + dot(t_put8[k, rows, :], t_lo8[k, :, lanes]) * t_down[:, at:at + 256])
            yield

    def f_prep(k, hi, lo):
        for at in range(0, cap, step):
            val = dot(f_pick[k, pl.ds(at, step), :], row_seg[...]) * coef_v[k, pl.ds(at, step), :].astype(f32)
            hi[pl.ds(at, step), :], lo[pl.ds(at, step), :] = split(val)
            yield

    def f_fill(k, hi, lo):
        p = f_put[k]
        parts = []
        for at in range(0, states, 256):
            lanes = pl.ds(at, 256)
            parts.append(jnp.concatenate(split(dot(p, hi[:, lanes]) + dot(p, lo[:, lanes])), axis=0))
            yield
        both = jnp.concatenate(parts, axis=1)
        for at in range(0, states, 256):
            lanes = pl.ds(at, 256)
            wide = dot(both, kern_v[k, :, lanes])
            col_part[:, lanes] += wide[:n_tgt] + wide[n_tgt:]
            yield

    bufs = [(hi_a, lo_a), (hi_b, lo_b)]
    tabs = [tab_a, tab_b]

    def hand(n, from_rows, to_rows):
        return pltpu.make_async_remote_copy(
            src_ref=row_seg.at[from_rows], dst_ref=row_seg.at[to_rows], send_sem=sent.at[2 + n],
            recv_sem=gather_half.at[n], device_id=sibling, device_id_type=MESH)

    hands = (hand(0, near_mine, near_other), hand(1, far_mine, far_other))

    zip_run(t_table(0, tab_a))
    zip_run(t_prep(0, tab_a), t_table(1, tab_b))
    for k in range(nk - 1):
        todo = [t_fill(k, pl.ds(near, 2 * far)), t_prep(k + 1, tabs[(k + 1) % 2])]
        if k + 2 < nk:
            todo.append(t_table(k + 2, tabs[k % 2]))
        zip_run(*todo)
        if k == 1:
            pltpu.make_async_copy(row_seg.at[near_mine], row_seg.at[near_mine], gather_row.at[0]).wait()
            pltpu.make_async_copy(row_seg.at[far_mine], row_seg.at[far_mine], gather_row.at[1]).wait()
            for copy in hands:
                copy.start()
    for copy in hands:
        copy.wait()
    first = f_prep(0, *bufs[0])
    for done in t_fill(nk - 1, far_other):
        next(first)

    swap = pltpu.make_async_remote_copy(
        src_ref=row_part.at[far_other], dst_ref=sibling_part, send_sem=sent.at[4], recv_sem=cross,
        device_id=sibling, device_id_type=MESH)
    swap.start()
    zip_run(t_fill(nk - 1, far_mine), first)

    zip_run(f_fill(0, *bufs[0]), f_prep(1, *bufs[1]))
    swap.wait()

    def code_row(i, z):
        at = pl.ds(pl.multiple_of(i * 64, 64), 64)
        row_code[at, :] = encode(row_part[pl.ds(pl.multiple_of(near + i * 64, 64), 64), :] + sibling_part[at, :])
        return z

    lax.fori_loop(0, far // 64, code_row, 0)

    def send_row(t, z):
        peer, spot = far_peer(t)
        pltpu.make_async_remote_copy(
            src_ref=row_code.at[piece(t)], dst_ref=row_land.at[piece(spot)],
            send_sem=sent.at[5], recv_sem=reduce_row, device_id={"col": peer}, device_id_type=MESH).start()
        return z

    lax.fori_loop(0, chips - LINE, send_row, 0)

    for k in range(1, nk - 1):
        zip_run(f_fill(k, *bufs[k % 2]), f_prep(k + 1, *bufs[(k + 1) % 2]))
    zip_run(f_fill(nk - 1, *bufs[(nk - 1) % 2]))

    col_code[...] = encode(col_part[...])

    def send_col(d, z):
        peer = row_peer(d)
        pltpu.make_async_remote_copy(
            src_ref=col_code.at[piece(peer)], dst_ref=col_land.at[piece(r)],
            send_sem=sent.at[6], recv_sem=reduce_col,
            device_id={"row": peer}, device_id_type=MESH).start()
        return z

    lax.fori_loop(1, n_row, send_col, 0)
    own = pltpu.make_async_copy(col_code.at[piece(r)], col_land.at[piece(r)], reduce_col)
    own.start()

    for k in range(nk):
        zip_run(t_fill(k, near_rows))
    near_code[...] = encode(row_part[near_rows, :])

    def send_near(d, z):
        x = lax.rem(at_x + d, LINE)
        pltpu.make_async_remote_copy(
            src_ref=near_code.at[piece(x)], dst_ref=near_land.at[piece(at_x)],
            send_sem=sent.at[7], recv_sem=reduce_near, device_id={"col": line_col(x, core)}, device_id_type=MESH).start()
        return z

    def send_near_across(x, z):
        pltpu.make_async_remote_copy(
            src_ref=near_code.at[piece(LINE + x)], dst_ref=near_land.at[piece(LINE + at_x)],
            send_sem=sent.at[7], recv_sem=reduce_near, device_id={"col": line_col(x, 1 - core)}, device_id_type=MESH).start()
        return z

    lax.fori_loop(1, LINE, send_near, 0)
    lax.fori_loop(0, LINE, send_near_across, 0)
    pltpu.make_async_copy(near_code.at[piece(at_x)], near_land.at[piece(at_x)], reduce_near).start()

    pltpu.make_async_copy(row_land, row_land, reduce_row).wait()
    total = decode(row_land[pl.ds(0, pb), :])
    for j in range(1, chips - LINE):
        total = total + decode(row_land[pl.ds(j * pb, pb), :])
    pltpu.make_async_copy(col_land, col_land, reduce_col).wait()
    for j in range(n_row):
        total = total + decode(col_land[pl.ds(j * pb, pb), :])
    pltpu.make_async_copy(near_land, near_land, reduce_near).wait()
    for j in range(2 * LINE):
        total = total + decode(near_land[pl.ds(j * pb, pb), :])
    out[...] = total

    for ref, n, sem in ((col_seg, n_row - 1, 0), (row_seg, chips - 1, 1), (row_land, chips - LINE, 5),
                        (col_land, n_row - 1, 6), (near_land, 2 * LINE - 1, 7)):
        gone = ref.at[pl.ds(0, n * pb)]
        pltpu.make_async_copy(gone, gone, sent.at[sem]).wait()


def shards(amplitudes, energies, kernels, coefficients, target_block, source_block, slot_count):
    pb, states = amplitudes.shape
    n_row = lax.axis_size("row")
    n_col = lax.axis_size("col")
    nk, cap = coefficients.shape[2:4]
    n_src, n_tgt = n_col * pb, n_row * pb
    n_far = n_src // 2 - LINE * pb
    vmem = pl.BlockSpec(memory_space=pltpu.VMEM)
    hbm = pl.BlockSpec(memory_space=pl.ANY)
    dma = pltpu.SemaphoreType.DMA
    total = pl.pallas_call(
        functools.partial(body, n_row, n_col),
        out_shape=pltpu.VMEM((pb, states), f32),
        in_specs=[hbm, hbm, hbm, hbm, hbm, pl.BlockSpec(memory_space=pltpu.SMEM)],
        out_specs=vmem,
        scratch_shapes=[
            pltpu.VMEM((nk, cap, states), bf16),
            pltpu.VMEM((nk, states, states), bf16),
            pltpu.VMEM((n_src, states), bf16),
            pltpu.VMEM((n_tgt, states), bf16),
            pltpu.VMEM((n_src, states), f32),
            pltpu.VMEM((n_tgt, states), f32),
            pltpu.VMEM((n_far, states), f32),
            pltpu.VMEM((n_far, states + LANES), i16),
            pltpu.VMEM((n_far, states + LANES), i16),
            pltpu.VMEM((n_src - 2 * n_far, states + LANES), i16),
            pltpu.VMEM((n_src - 2 * n_far, states + LANES), i16),
            pltpu.VMEM((n_tgt, states + LANES), i16),
            pltpu.VMEM((n_tgt, states + LANES), i16),
            pltpu.VMEM((nk, cap, n_tgt), bf16),
            pltpu.VMEM((nk, n_src, cap), bf16),
            pltpu.VMEM((nk, n_src, cap), f8),
            pltpu.VMEM((nk, cap, n_src), bf16),
            pltpu.VMEM((nk, n_tgt, cap), bf16),
            pltpu.VMEM((nk, cap, states), bf16),
            pltpu.VMEM((nk, cap, states), f8),
            pltpu.VMEM((cap, states), bf16),
            pltpu.VMEM((cap, states), bf16),
            pltpu.VMEM((cap, states), bf16),
            pltpu.VMEM((cap, states), bf16),
            pltpu.VMEM((nk, states, states), bf16),
            pltpu.VMEM((2 * n_tgt, states), bf16),
            pltpu.VMEM((2 * n_tgt, states), bf16),
            pltpu.VMEM((nk * cap // LANES, LANES), i32),
            pltpu.VMEM((nk * cap // LANES, LANES), i32),
            dma((2, nk)), dma((2,)), dma((2,)), dma((2,)), dma, dma, dma, dma, dma, dma((8,)),
        ],
        compiler_params=pltpu.CompilerParams(
            collective_id=0, has_side_effects=True, vmem_limit_bytes=60 * 1024 * 1024),
        name="couplings",
    )(amplitudes, coefficients.reshape(nk, cap, states), kernels,
      target_block.reshape(nk * cap // LANES, LANES), source_block.reshape(nk * cap // LANES, LANES),
      slot_count.reshape(nk))
    return total + energies * amplitudes.astype(f32)


def solution(mesh):
    in_specs = (
        P(("row", "col"), None),
        P(("row", "col"), None),
        P(),
        P("row", "col", None, None, None),
        P("row", "col", None, None),
        P("row", "col", None, None),
        P("row", "col", None),
    )
    out_specs = P(("row", "col"), None)
    return jax.shard_map(shards, mesh=mesh, in_specs=in_specs, out_specs=out_specs, check_vma=False)
```

```python
import functools
import jax
import jax.numpy as jnp
from jax import lax
from jax.experimental import pallas as pl
from jax.experimental.pallas import tpu as pltpu
from jax.sharding import PartitionSpec as P

MESH = pl.DeviceIdType.MESH
f32, bf16, i32, i16, f8 = jnp.float32, jnp.bfloat16, jnp.int32, jnp.int16, jnp.float8_e5m2
LANES = 128
LINE = 4


def split(x):
    hi = x.astype(bf16)
    return hi, (x - hi.astype(f32)).astype(bf16)


def dot(a, b):
    return jnp.dot(a, b, preferred_element_type=f32)


def level(x):
    top = jnp.max(jnp.max(jnp.abs(x.astype(f32)), axis=0, keepdims=True), axis=1, keepdims=True)
    top = jnp.maximum(jnp.broadcast_to(top, (1, x.shape[1])), 1e-30)
    return jnp.ceil(jnp.log2(top * 0.125))


def encode(x):
    states = x.shape[1]
    top = jnp.maximum(jnp.max(jnp.abs(x), axis=1, keepdims=True), 1e-30)
    power = jnp.ceil(jnp.log2(jnp.broadcast_to(top, (x.shape[0], LANES)) * (1.0 / 32000.0)))
    scale = jnp.exp2(-power)
    parts = [jnp.round(x[:, at:at + LANES] * scale).astype(i32).astype(i16) for at in range(0, states, LANES)]
    return jnp.concatenate(parts + [power.astype(i32).astype(i16)], axis=1)


def decode(coded):
    states = coded.shape[1] - LANES
    scale = jnp.exp2(coded[:, states:].astype(i32).astype(f32))
    parts = [coded[:, at:at + LANES].astype(i32).astype(f32) * scale for at in range(0, states, LANES)]
    return jnp.concatenate(parts, axis=1)


def build(idx, cnt, k, rows_ref, cols_ref, count, rows8_ref=None):
    one, zero = jnp.bfloat16(1), jnp.bfloat16(0)
    for m in range(idx.shape[0]):
        lane = lax.broadcasted_iota(i32, (1, LANES), 1) + m * LANES
        row = jnp.where(lane < cnt[k], idx[m:m + 1, :], -1)
        wide = jnp.broadcast_to(row, (LANES, LANES))
        down, across = wide.astype(i16), wide.T.astype(i16)
        for base in range(0, count, LANES):
            it = lax.broadcasted_iota(i16, (LANES, LANES), 0)
            hot = jnp.where(it == down - jnp.int16(base), one, zero)
            rows_ref[k, pl.ds(base, LANES), pl.ds(m * LANES, LANES)] = hot
            if rows8_ref is not None:
                rows8_ref[k, pl.ds(base, LANES), pl.ds(m * LANES, LANES)] = hot.astype(f8)
            it = lax.broadcasted_iota(i16, (LANES, LANES), 1)
            cols_ref[k, pl.ds(m * LANES, LANES), pl.ds(base, LANES)] = jnp.where(it == across - jnp.int16(base), one, zero)


def zip_run(*gens):
    gens = list(gens)
    while gens:
        for g in list(gens):
            try:
                next(g)
            except StopIteration:
                gens.remove(g)


def body(n_row, n_col, amp, coef, kern, tgt_hbm, src_hbm, cnt_hbm, out,
         coef_v, kern_v, row_seg, col_seg, row_part, col_part, sibling_part,
         row_code, row_land, near_code, near_land, col_code, col_land,
         t_pick, t_put, t_put8, f_pick, f_put, t_hi, t_lo8, hi_a, lo_a, hi_b, lo_b,
         kern_t, tab_a, tab_b, tgt, src, cnt,
         load_sem, index_sem, gather_row, gather_half, gather_col, cross, reduce_row, reduce_near, reduce_col, sent):
    r = lax.axis_index("row")
    c = lax.axis_index("col")
    core = lax.rem(c, 2)
    chip = lax.div(c, 2)
    chips = n_col // 2
    nk, cap, states = coef_v.shape
    pb = amp.shape[0]
    n_src, n_tgt = n_col * pb, n_row * pb
    lines = chips // LINE
    line, at_x = lax.div(chip, LINE), lax.rem(chip, LINE)
    near = 2 * LINE * pb
    far = (chips - LINE) * pb
    near_mine, near_other = pl.ds(0, near // 2), pl.ds(near // 2, near // 2)
    far_mine, far_other = pl.ds(near, far), pl.ds(near + far, far)
    near_rows = pl.ds(0, near)
    groups = cap // LANES
    sibling = {"col": c + 1 - 2 * core}

    def piece(at):
        return pl.ds(pl.multiple_of(at * pb, pb), pb)

    def load(k):
        return (pltpu.make_async_copy(kern.at[k], kern_v.at[k], load_sem.at[0, k]),
                pltpu.make_async_copy(coef.at[k], coef_v.at[k], load_sem.at[1, k]))

    def chip_peer(d):
        return lax.rem(chip + d, chips)

    def row_peer(d):
        return lax.rem(r + d, n_row)

    def line_col(x, q):
        return (line * LINE + x) * 2 + q

    def far_peer(t):
        ahead = lax.div(t, LINE) + 1
        there = lax.rem(line + ahead, lines)
        return (there * LINE + lax.rem(t, LINE)) * 2 + core, (lines - ahead - 1) * LINE + at_x

    barrier = pltpu.get_barrier_semaphore()

    def greet_row(d, z):
        pl.semaphore_signal(barrier, inc=1, device_id={"row": row_peer(d)}, device_id_type=MESH)
        return z

    def greet_chip(d, z):
        pl.semaphore_signal(barrier, inc=1, device_id={"col": chip_peer(d) * 2 + core}, device_id_type=MESH)
        return z

    lax.fori_loop(1, n_row, greet_row, 0)
    lax.fori_loop(1, chips, greet_chip, 0)

    def greet_line(x, z):
        pl.semaphore_signal(barrier, inc=1, device_id={"col": line_col(x, 1 - core)}, device_id_type=MESH)
        return z

    lax.fori_loop(0, LINE, greet_line, 0)

    indices = (pltpu.make_async_copy(tgt_hbm, tgt, index_sem.at[0]),
               pltpu.make_async_copy(src_hbm, src, index_sem.at[1]),
               pltpu.make_async_copy(cnt_hbm, cnt, index_sem.at[2]))
    for copy in indices:
        copy.start()
    for k in range(nk):
        for copy in load(k):
            copy.start()
    own_row = pltpu.make_async_copy(amp, row_seg.at[piece(at_x)], gather_row.at[0])
    own_col = pltpu.make_async_copy(amp, col_seg.at[piece(r)], gather_col)
    own_col.start()
    own_row.start()

    pl.semaphore_wait(barrier, n_row + chips + LINE - 2)

    def send_col_amp(d, z):
        pltpu.make_async_remote_copy(
            src_ref=amp, dst_ref=col_seg.at[piece(r)], send_sem=sent.at[0], recv_sem=gather_col,
            device_id={"row": row_peer(d)}, device_id_type=MESH).start()
        return z

    def send_near_amp(d, z):
        pltpu.make_async_remote_copy(
            src_ref=amp, dst_ref=row_seg.at[piece(at_x)], send_sem=sent.at[1], recv_sem=gather_row.at[0],
            device_id={"col": line_col(lax.rem(at_x + d, LINE), core)}, device_id_type=MESH).start()
        return z

    def send_far_amp(t, z):
        peer, spot = far_peer(t)
        pltpu.make_async_remote_copy(
            src_ref=amp, dst_ref=row_seg.at[piece(2 * LINE + spot)], send_sem=sent.at[1], recv_sem=gather_row.at[1],
            device_id={"col": peer}, device_id_type=MESH).start()
        return z

    lax.fori_loop(1, n_row, send_col_amp, 0)
    lax.fori_loop(1, LINE, send_near_amp, 0)
    lax.fori_loop(0, chips - LINE, send_far_amp, 0)

    for copy in indices:
        copy.wait()

    def build_both(k, z):
        at = pl.ds(pl.multiple_of(k * groups, groups), groups)
        build(tgt[at, :], cnt, k, f_put, t_pick, n_tgt)
        j = src[at, :]
        piece_of = lax.shift_right_logical(j, 4)
        swapped = (piece_of & 1) ^ core
        of_line = lax.shift_right_logical(piece_of, 1)
        ahead = (lax.shift_right_logical(of_line, 2) - line + lines) & (lines - 1)
        x = of_line & (LINE - 1)
        spot = jnp.where(ahead == 0, swapped * (near // 2) + x * pb,
                         near + swapped * far + ((ahead - 1) * LINE + x) * pb) + (j & (pb - 1))
        build(spot, cnt, k, t_put, f_pick, n_src, t_put8)
        return z

    lax.fori_loop(0, nk, build_both, 0)
    row_part[...] = jnp.zeros_like(row_part)
    col_part[...] = jnp.zeros_like(col_part)
    for k in range(nk):
        for copy in load(k):
            copy.wait()

    def turn(k, z):
        kern_t[k] = kern_v[k].T
        return z

    lax.fori_loop(0, nk, turn, 0)
    pltpu.make_async_copy(col_seg, col_seg, gather_col).wait()

    step = cap // 4
    t_level = level(col_seg[...])
    t_up, t_down = jnp.exp2(14.0 - t_level), jnp.exp2(t_level - 14.0)

    def t_table(k, tab):
        h, l = split(dot(col_seg[...], kern_t[k]))
        tab[pl.ds(0, n_tgt), :] = h
        tab[pl.ds(n_tgt, n_tgt), :] = l
        yield

    def t_prep(k, tab):
        both = tab[...]
        for at in range(0, cap, step):
            p = t_pick[k, pl.ds(at, step), :]
            val = dot(jnp.concatenate([p, p], axis=1), both) * coef_v[k, pl.ds(at, step), :].astype(f32)
            h = val.astype(bf16)
            t_hi[k, pl.ds(at, step), :] = h
            t_lo8[k, pl.ds(at, step), :] = ((val - h.astype(f32)) * t_up).astype(f8)
            yield

    def t_fill(k, rows):
        for at in range(0, states, 256):
            lanes = pl.ds(at, 256)
            row_part[rows, lanes] += (dot(t_put[k, rows, :], t_hi[k, :, lanes])
                                      + dot(t_put8[k, rows, :], t_lo8[k, :, lanes]) * t_down[:, at:at + 256])
            yield

    def f_prep(k, hi, lo):
        for at in range(0, cap, step):
            val = dot(f_pick[k, pl.ds(at, step), :], row_seg[...]) * coef_v[k, pl.ds(at, step), :].astype(f32)
            hi[pl.ds(at, step), :], lo[pl.ds(at, step), :] = split(val)
            yield

    def f_fill(k, hi, lo):
        p = f_put[k]
        parts = []
        for at in range(0, states, 256):
            lanes = pl.ds(at, 256)
            parts.append(jnp.concatenate(split(dot(p, hi[:, lanes]) + dot(p, lo[:, lanes])), axis=0))
            yield
        both = jnp.concatenate(parts, axis=1)
        for at in range(0, states, 256):
            lanes = pl.ds(at, 256)
            wide = dot(both, kern_v[k, :, lanes])
            col_part[:, lanes] += wide[:n_tgt] + wide[n_tgt:]
            yield

    bufs = [(hi_a, lo_a), (hi_b, lo_b)]
    tabs = [tab_a, tab_b]

    def hand(n, from_rows, to_rows):
        return pltpu.make_async_remote_copy(
            src_ref=row_seg.at[from_rows], dst_ref=row_seg.at[to_rows], send_sem=sent.at[2 + n],
            recv_sem=gather_half.at[n], device_id=sibling, device_id_type=MESH)

    hands = (hand(0, near_mine, near_other), hand(1, far_mine, far_other))

    zip_run(t_table(0, tab_a))
    zip_run(t_prep(0, tab_a), t_table(1, tab_b))
    for k in range(nk - 1):
        todo = [t_fill(k, pl.ds(near, 2 * far)), t_prep(k + 1, tabs[(k + 1) % 2])]
        if k + 2 < nk:
            todo.append(t_table(k + 2, tabs[k % 2]))
        zip_run(*todo)
        if k == 1:
            pltpu.make_async_copy(row_seg.at[near_mine], row_seg.at[near_mine], gather_row.at[0]).wait()
            pltpu.make_async_copy(row_seg.at[far_mine], row_seg.at[far_mine], gather_row.at[1]).wait()
            for copy in hands:
                copy.start()
    for copy in hands:
        copy.wait()
    first = f_prep(0, *bufs[0])
    for done in t_fill(nk - 1, far_other):
        next(first)

    swap = pltpu.make_async_remote_copy(
        src_ref=row_part.at[far_other], dst_ref=sibling_part, send_sem=sent.at[4], recv_sem=cross,
        device_id=sibling, device_id_type=MESH)
    swap.start()
    zip_run(t_fill(nk - 1, far_mine), first)

    zip_run(f_fill(0, *bufs[0]), f_prep(1, *bufs[1]))
    swap.wait()

    def code_row(i, z):
        at = pl.ds(pl.multiple_of(i * 64, 64), 64)
        row_code[at, :] = encode(row_part[pl.ds(pl.multiple_of(near + i * 64, 64), 64), :] + sibling_part[at, :])
        return z

    lax.fori_loop(0, far // 64, code_row, 0)

    def send_row(t, z):
        peer, spot = far_peer(t)
        pltpu.make_async_remote_copy(
            src_ref=row_code.at[piece(t)], dst_ref=row_land.at[piece(spot)],
            send_sem=sent.at[5], recv_sem=reduce_row, device_id={"col": peer}, device_id_type=MESH).start()
        return z

    lax.fori_loop(0, chips - LINE, send_row, 0)

    for k in range(1, nk - 1):
        zip_run(f_fill(k, *bufs[k % 2]), f_prep(k + 1, *bufs[(k + 1) % 2]))
    zip_run(f_fill(nk - 1, *bufs[(nk - 1) % 2]))

    col_code[...] = encode(col_part[...])

    def send_col(d, z):
        peer = row_peer(d)
        pltpu.make_async_remote_copy(
            src_ref=col_code.at[piece(peer)], dst_ref=col_land.at[piece(r)],
            send_sem=sent.at[6], recv_sem=reduce_col,
            device_id={"row": peer}, device_id_type=MESH).start()
        return z

    lax.fori_loop(1, n_row, send_col, 0)
    own = pltpu.make_async_copy(col_code.at[piece(r)], col_land.at[piece(r)], reduce_col)
    own.start()

    for k in range(nk):
        zip_run(t_fill(k, near_rows))
    near_code[...] = encode(row_part[near_rows, :])

    def send_near(d, z):
        x = lax.rem(at_x + d, LINE)
        pltpu.make_async_remote_copy(
            src_ref=near_code.at[piece(x)], dst_ref=near_land.at[piece(at_x)],
            send_sem=sent.at[7], recv_sem=reduce_near, device_id={"col": line_col(x, core)}, device_id_type=MESH).start()
        return z

    def send_near_across(x, z):
        pltpu.make_async_remote_copy(
            src_ref=near_code.at[piece(LINE + x)], dst_ref=near_land.at[piece(LINE + at_x)],
            send_sem=sent.at[7], recv_sem=reduce_near, device_id={"col": line_col(x, 1 - core)}, device_id_type=MESH).start()
        return z

    lax.fori_loop(1, LINE, send_near, 0)
    lax.fori_loop(0, LINE, send_near_across, 0)
    pltpu.make_async_copy(near_code.at[piece(at_x)], near_land.at[piece(at_x)], reduce_near).start()

    pltpu.make_async_copy(row_land, row_land, reduce_row).wait()
    total = decode(row_land[pl.ds(0, pb), :])
    for j in range(1, chips - LINE):
        total = total + decode(row_land[pl.ds(j * pb, pb), :])
    pltpu.make_async_copy(col_land, col_land, reduce_col).wait()
    for j in range(n_row):
        total = total + decode(col_land[pl.ds(j * pb, pb), :])
    pltpu.make_async_copy(near_land, near_land, reduce_near).wait()
    for j in range(2 * LINE):
        total = total + decode(near_land[pl.ds(j * pb, pb), :])
    out[...] = total

    for ref, n, sem in ((col_seg, n_row - 1, 0), (row_seg, chips - 1, 1), (row_land, chips - LINE, 5),
                        (col_land, n_row - 1, 6), (near_land, 2 * LINE - 1, 7)):
        gone = ref.at[pl.ds(0, n * pb)]
        pltpu.make_async_copy(gone, gone, sent.at[sem]).wait()


def shards(amplitudes, energies, kernels, coefficients, target_block, source_block, slot_count):
    pb, states = amplitudes.shape
    n_row = lax.axis_size("row")
    n_col = lax.axis_size("col")
    nk, cap = coefficients.shape[2:4]
    n_src, n_tgt = n_col * pb, n_row * pb
    n_far = n_src // 2 - LINE * pb
    vmem = pl.BlockSpec(memory_space=pltpu.VMEM)
    hbm = pl.BlockSpec(memory_space=pl.ANY)
    dma = pltpu.SemaphoreType.DMA
    total = pl.pallas_call(
        functools.partial(body, n_row, n_col),
        out_shape=pltpu.VMEM((pb, states), f32),
        in_specs=[hbm] * 6,
        out_specs=vmem,
        scratch_shapes=[
            pltpu.VMEM((nk, cap, states), bf16),
            pltpu.VMEM((nk, states, states), bf16),
            pltpu.VMEM((n_src, states), bf16),
            pltpu.VMEM((n_tgt, states), bf16),
            pltpu.VMEM((n_src, states), f32),
            pltpu.VMEM((n_tgt, states), f32),
            pltpu.VMEM((n_far, states), f32),
            pltpu.VMEM((n_far, states + LANES), i16),
            pltpu.VMEM((n_far, states + LANES), i16),
            pltpu.VMEM((n_src - 2 * n_far, states + LANES), i16),
            pltpu.VMEM((n_src - 2 * n_far, states + LANES), i16),
            pltpu.VMEM((n_tgt, states + LANES), i16),
            pltpu.VMEM((n_tgt, states + LANES), i16),
            pltpu.VMEM((nk, cap, n_tgt), bf16),
            pltpu.VMEM((nk, n_src, cap), bf16),
            pltpu.VMEM((nk, n_src, cap), f8),
            pltpu.VMEM((nk, cap, n_src), bf16),
            pltpu.VMEM((nk, n_tgt, cap), bf16),
            pltpu.VMEM((nk, cap, states), bf16),
            pltpu.VMEM((nk, cap, states), f8),
            pltpu.VMEM((cap, states), bf16),
            pltpu.VMEM((cap, states), bf16),
            pltpu.VMEM((cap, states), bf16),
            pltpu.VMEM((cap, states), bf16),
            pltpu.VMEM((nk, states, states), bf16),
            pltpu.VMEM((2 * n_tgt, states), bf16),
            pltpu.VMEM((2 * n_tgt, states), bf16),
            pltpu.VMEM((nk * cap // LANES, LANES), i32),
            pltpu.VMEM((nk * cap // LANES, LANES), i32),
            pltpu.SMEM((nk,), i32),
            dma((2, nk)), dma((3,)), dma((2,)), dma((2,)), dma, dma, dma, dma, dma, dma((8,)),
        ],
        compiler_params=pltpu.CompilerParams(
            collective_id=0, has_side_effects=True, vmem_limit_bytes=60 * 1024 * 1024),
        name="couplings",
    )(amplitudes, coefficients.reshape(nk, cap, states), kernels,
      target_block.reshape(nk * cap // LANES, LANES), source_block.reshape(nk * cap // LANES, LANES),
      slot_count.reshape(nk))
    return total + energies * amplitudes.astype(f32)


def solution(mesh):
    in_specs = (
        P(("row", "col"), None),
        P(("row", "col"), None),
        P(),
        P("row", "col", None, None, None),
        P("row", "col", None, None),
        P("row", "col", None, None),
        P("row", "col", None),
    )
    out_specs = P(("row", "col"), None)
    return jax.shard_map(shards, mesh=mesh, in_specs=in_specs, out_specs=out_specs, check_vma=False)
```
